256 devices in a mesh: section: 4 (over z_hi), seq: 64 (over z_lo, x, y, core).
Axes of the slice: x: 4, y: 4, z: 8 (z_hi: 4, z_lo: 2; z = z_hi * 2 + z_lo), core: 2. Of those that a mesh axis runs over, the one named last changes fastest.
Arguments:
- prompt: bfloat16 [32768, 7168], P('seq', 'section'), may hold values from -6 to 6
- kv_down: bfloat16 [7168, 576], P('section'), may hold values from -0.0625 to 0.0625
- latent_gain: float32 [512], replicated, may hold values from 0.1 to 1.9
- block_home: int32 [256], P('seq'), may hold values from 0 to 7, as said below
- block_slot: int32 [256], P('seq'), may hold values from 0 to 1, as said below
- latent_cache: bfloat16 [8, 16384, 576], P('section', 'seq'), may hold values from -6 to 6
- cache_lengths: int32 [8], P('section'), may hold values from 2 to 16384, as said below
- queries: bfloat16 [8, 128, 2, 576], P('section'), may hold values from -70 to 70
- new_rows: bfloat16 [8, 2, 576], P('section'), may hold values from -12 to 12
Outputs:
- attended: bfloat16 [8, 128, 2, 512], P('section', 'seq')
The draws below stay inside these ranges and needn't reach their ends.
Inputs may be any that keep to these rules, and one draw needn't show every extreme that they name: Group of a block is block_home // 2. Of the 4 blocks of one seq index, exactly 2 go to one group and at most 2 to any group. No two blocks of one seq index share both home and slot. At seq index 0 no block has slot 0. `block_slot`: see block_home. `cache_lengths`: some home has all 16384 positions live.
All inputs are finite; a program needn't handle non-finite values.
Results may differ from the reference program's by a relative error of at most 0.006.
Values sent between devices are 32-bit elements; how exact they have to be, the bound alone decides.
A program may use at most 192 MiB of HBM per device.

```python
import jax
import jax.numpy as jnp
from jax import lax

D = 7168
LAT = 512
ROPE = 64
HEADS = 128
WIDE = 576
BLK = 128
NEW = 2
PTOK = 512
CSLOT = 256
REQ = 2
TOKENS = 32768
CTX = 16384
NH = 8
N_SECTION = 4
N_SEQ = 64


def block_plan(key):
    key = jax.random.fold_in(key, 101)
    key_a, key_b, key_c, key_d = jax.random.split(key, 4)
    per_column = PTOK // BLK
    capacity = per_column // 2
    sub_blocks = CSLOT // BLK
    busiest = jax.random.randint(key_a, (N_SEQ,), 0, N_SECTION)
    others = (busiest[:, None] + 1 + jax.random.randint(key_b, (N_SEQ, per_column), 0, N_SECTION - 1)) % N_SECTION
    shuffle = jnp.argsort(jax.random.randint(key_c, (N_SEQ, per_column), 0, 1 << 16) * per_column + jnp.arange(per_column)[None, :], axis=1)
    ranks_in = jnp.argsort(shuffle, axis=1)
    groups = jnp.where(ranks_in < capacity, busiest[:, None], others).astype(jnp.int32)
    same_group = groups[:, :, None] == groups[:, None, :]
    earlier = jnp.arange(per_column)[None, :] < jnp.arange(per_column)[:, None]
    ranks = jnp.sum(same_group & earlier[None], axis=2).astype(jnp.int32)
    slot_total = REQ * sub_blocks
    slot_ids = jnp.arange(slot_total)
    scores = jax.random.randint(key_d, (N_SEQ, N_SECTION, slot_total), 0, 1 << 12) * slot_total + slot_ids[None, None, :]
    barred = (jnp.arange(N_SEQ) == 0)[:, None, None] & (slot_ids % sub_blocks == 0)[None, None, :]
    scores = scores + jnp.where(barred, (1 << 12) * slot_total, 0)
    listing = jnp.argsort(scores, axis=2).astype(jnp.int32)
    picked = listing[jnp.arange(N_SEQ)[:, None], groups]
    chosen = jnp.take_along_axis(picked, ranks[..., None], axis=2)[..., 0]
    homes = groups * REQ + chosen // sub_blocks
    slots = chosen % sub_blocks
    return (homes.reshape(-1).astype(jnp.int32), slots.reshape(-1).astype(jnp.int32))


def draw_block_home(key, part):
    return block_plan(key)[0]


def draw_block_slot(key, part):
    return block_plan(key)[1]


def draw_cache_lengths(key, part):
    key = jax.random.fold_in(key, 3)
    key_a, key_b = jax.random.split(key)
    lengths = jax.random.randint(key_a, (NH,), 2, CTX + 1)
    chosen = jax.random.randint(key_b, (), 0, NH)
    return jnp.where(jnp.arange(NH) == chosen, CTX, lengths).astype(jnp.int32)


def draw_latent_cache(key, part):
    key = jax.random.fold_in(key, 5)
    key_a = jax.random.fold_in(key, 0)
    values = jnp.clip(jax.random.normal(key_a, (NH, CTX, LAT + ROPE), jnp.float32), -6.0, 6.0)
    return values.astype(jnp.bfloat16)


def draw_queries(key, part):
    key = jax.random.fold_in(key, 7)
    values = jnp.clip(jax.random.normal(key, (NH, HEADS, NEW, LAT + ROPE), jnp.float32), -6.0, 6.0) * 1.6
    return values.astype(jnp.bfloat16)


def block_levels(stream_key, dims, cuts, smallest, largest):
    loudness = 1.0
    for axis_at, blocks in cuts:
        heights = jax.random.uniform(jax.random.fold_in(jax.random.fold_in(stream_key, 6), axis_at), (blocks,), jnp.float32, smallest / len(cuts), largest / len(cuts))
        loudness = loudness * jnp.repeat(jnp.exp(heights), dims[axis_at] // blocks).reshape((-1,) + (1,) * (len(dims) - 1 - axis_at))
    return loudness


def bell_draw(own_key, dims, scale, most, shards=(), kind=jnp.bfloat16):
    loudness = block_levels(own_key, dims, shards, -0.22, 0.18) if shards else 1.0
    drawn = jax.random.normal(own_key, dims, jnp.float32) * scale * loudness
    return jnp.minimum(jnp.maximum(drawn, -most), most).astype(kind)


def setup_inputs(seed: int = 0) -> dict:
    keys = jax.random.split(jax.random.key(seed), 10)
    prompt = bell_draw(keys[0], (TOKENS, D), 1.0, 6.0, ((0, 64), (1, 4)))
    kv_down = bell_draw(keys[1], (D, WIDE), D ** -0.5, 0.0625, ((0, 4),))
    latent_gain = jnp.clip(1.0 + 0.18 * jax.random.normal(keys[2], (LAT,), jnp.float32), 0.1, 1.9)
    block_home = draw_block_home(jax.random.fold_in(keys[9], 71), 0)
    block_slot = draw_block_slot(jax.random.fold_in(keys[9], 71), 0)
    latent_cache = draw_latent_cache(jax.random.fold_in(keys[9], 71), 0)
    cache_lengths = draw_cache_lengths(jax.random.fold_in(keys[9], 71), 0)
    queries = draw_queries(jax.random.fold_in(keys[9], 71), 0)
    new_rows = bell_draw(keys[8], (NH, NEW, WIDE), 2.0, 12.0, ((0, 4),))
    return {"prompt": prompt, "kv_down": kv_down, "latent_gain": latent_gain, "block_home": block_home, "block_slot": block_slot, "latent_cache": latent_cache, "cache_lengths": cache_lengths, "queries": queries, "new_rows": new_rows}


score_scale = 192.0 ** (-0.5)
epsilon = 1e-06
rope_base = 10000.0
big_value = 1e+30

def make_rows(projected, position, latent_gain):
    latent = projected[..., :LAT]
    mean_square = lax.optimization_barrier(jnp.mean(latent * latent, axis=-1, keepdims=True))
    latent = latent * lax.rsqrt(mean_square + epsilon) * latent_gain
    rotary = projected[..., LAT:]
    half_width = rotary.shape[-1] // 2
    inverse = rope_base ** (-2.0 * jnp.arange(half_width, dtype=jnp.float32) / (2 * half_width))
    angles = position[..., None] * inverse
    first_half = rotary[..., :half_width]
    second_half = rotary[..., half_width:]
    cosine_values = jnp.cos(angles)
    sine_values = jnp.sin(angles)
    turned = jnp.concatenate([first_half * cosine_values - second_half * sine_values, first_half * sine_values + second_half * cosine_values], axis=-1)
    return jnp.concatenate([latent, turned], axis=-1).astype(jnp.bfloat16)

def reference(prompt, kv_down, latent_gain, block_home, block_slot, latent_cache, cache_lengths, queries, new_rows):
    projected = jnp.dot(prompt, kv_down, preferred_element_type=jnp.float32)
    block_count = block_home.shape[0]
    projected = projected.reshape(block_count, BLK, LAT + ROPE)
    column_of = (jnp.arange(block_count, dtype=jnp.int32) // (PTOK // BLK)).astype(jnp.int32)
    first_pos = column_of * CSLOT + block_slot * BLK
    position = (first_pos[:, None] + jnp.arange(BLK, dtype=jnp.int32)[None, :]).astype(jnp.float32)
    fresh = make_rows(projected, position, latent_gain)
    block_target = (column_of * (CSLOT // BLK) + block_slot).astype(jnp.int32)
    causal = jnp.arange(NEW)[:, None] >= jnp.arange(NEW)[None, :]
    segments = CTX // CSLOT

    def one_home(home_index):
        targets = jnp.where(block_home == home_index, block_target, CTX // BLK).astype(jnp.int32)
        blocks = latent_cache[home_index].reshape(CTX // BLK, BLK, LAT + ROPE)
        blocks = blocks.at[targets].set(fresh, mode='drop')
        key_rows = blocks.reshape(CTX, LAT + ROPE).astype(jnp.float32)
        written = jnp.zeros((CTX // BLK,), jnp.int32).at[targets].set(1, mode='drop')
        alive = (jnp.arange(CTX, dtype=jnp.int32) < cache_lengths[home_index]) | (jnp.repeat(written, BLK) > 0)
        query_rows = queries[home_index].astype(jnp.float32)
        own_rows = new_rows[home_index].astype(jnp.float32)
        scores = jnp.einsum('knw,pw->knp', query_rows, key_rows) * score_scale
        own_scores = jnp.einsum('knw,mw->knm', query_rows, own_rows) * score_scale
        scores = jnp.where(alive[None, None, :], scores, -big_value)
        own_scores = jnp.where(causal[None], own_scores, -big_value)
        seg_scores = scores.reshape(HEADS, NEW, segments, CSLOT)
        seg_alive = alive.reshape(segments, CSLOT)
        seg_top = lax.optimization_barrier(jnp.max(seg_scores, axis=-1))
        weight = jnp.where(seg_alive[None, None], jnp.exp(seg_scores - seg_top[..., None]), 0.0).astype(jnp.bfloat16)
        seg_totals = lax.optimization_barrier(jnp.sum(weight.astype(jnp.float32), axis=-1))
        seg_numerator = jnp.einsum('kncp,cpl->kncl', weight.astype(jnp.float32), key_rows[:, :LAT].reshape(segments, CSLOT, LAT))
        row_top = jnp.maximum(lax.optimization_barrier(jnp.max(seg_top, axis=-1)), lax.optimization_barrier(jnp.max(own_scores, axis=-1)))
        factor = jnp.exp(seg_top - row_top[..., None])
        own_weight = jnp.where(causal[None], jnp.exp(own_scores - row_top[..., None]), 0.0).astype(jnp.bfloat16)
        totals = lax.optimization_barrier(jnp.sum(factor * seg_totals, axis=-1)) + lax.optimization_barrier(jnp.sum(own_weight.astype(jnp.float32), axis=-1))
        numerator = jnp.einsum('knc,kncl->knl', factor, seg_numerator)
        numerator = numerator + jnp.einsum('knm,ml->knl', own_weight.astype(jnp.float32), own_rows[:, :LAT])
        return (numerator / totals[..., None]).astype(jnp.bfloat16)
    return lax.map(one_home, jnp.arange(NH, dtype=jnp.int32))
```

```python
import functools

import jax
import jax.numpy as jnp
import numpy as np
from jax import lax
from jax.experimental import pallas as pl
from jax.experimental.pallas import tpu as pltpu
from jax.sharding import PartitionSpec as P

MESH = pl.DeviceIdType.MESH
LAT = 512
BLK = 128
CSLOT = 256
SCALE = 192.0 ** (-0.5)
EPS = 1e-6
BIG = 1e30

ROWS = 16
NCH = BLK // ROWS
LAG = 2
MSGS = 2 * NCH + LAG
PIECE = 9
TABLE = MSGS + 2 * NCH


def chunk_id(block, chunk):
    half = NCH // 2
    return (chunk // half) * (4 * half) + block * half + chunk % half


def passes(rel):
    n_right, n_left = rel.count(1), rel.count(3)
    opposite = [b for b in range(4) if rel[b] == 2]
    if len(opposite) == 1:
        right = 1 if n_right <= n_left else 0
    else:
        right = 1 + (n_left == 2) - (n_right == 2)
    right = min(max(right, 0), len(opposite))
    return opposite[:right], opposite[right:]


def lane_plan(rel, side):
    near, step = (1, 1) if side == 0 else (3, -1)
    mine = passes(rel)[side]
    behind = passes([(r + step) % 4 for r in rel])[side]
    plain = [b for b in range(4) if rel[b] == near and b not in behind]
    spots = {}
    if len(mine) == 2:
        for i in range(2 * NCH):
            spots[i] = (mine[i % 2], i // 2, 0)
        return spots
    if len(behind) == 2:
        for i in range(2 * NCH):
            spots[i + LAG] = (behind[i % 2], i // 2, 1)
        return spots
    early = [2 * LAG * (i // LAG) + i % LAG for i in range(NCH)]
    late = [e + LAG for e in early]
    if behind:
        for i in range(NCH):
            spots[late[i]] = (behind[0], i, 1)
    if mine:
        for i in range(NCH):
            spots[early[i]] = (mine[0], i, 0)
    free = ([] if mine else [early]) + ([] if behind else [late])
    for b, where in zip(plain, free):
        for i in range(NCH):
            spots[where[i]] = (b, i, 0)
    return spots


@functools.lru_cache(None)
def plan_table():
    table = np.zeros((256, TABLE), np.int32)
    for code in range(256):
        rel = [(code >> (2 * b)) & 3 for b in range(4)]
        if max(rel.count(g) for g in range(4)) > 2:
            continue
        for side in range(2):
            for m, (b, j, adds) in lane_plan(rel, side).items():
                table[code, m] |= (chunk_id(b, j) | (adds << 5)) << (6 * side)
        owned = [b for b in range(4) if rel[b] == 0]
        from_left = lane_plan([(r + 1) % 4 for r in rel], 0)
        from_right = lane_plan([(r - 1) % 4 for r in rel], 1)
        for k, b in enumerate(owned):
            for j in range(NCH):
                at_left = [m for m, v in from_left.items() if v[:2] == (b, j)][0]
                at_right = [m for m, v in from_right.items() if v[:2] == (b, j)][0]
                table[code, MSGS + k * NCH + j] = chunk_id(b, j) | (at_left << 5) | (at_right << 10)
    return table.reshape(-1)


@functools.lru_cache(None)
def turn_tables():
    lane = np.arange(128)
    inverse = 10000.0 ** (-2.0 * (lane % 32) / 64.0)
    base = (np.arange(128) * 128.0)[:, None] * inverse[None, :]
    row = np.arange(8 * NCH)
    inside = ((row // 8) * 16 + row % 8)[:, None] + np.where(lane < 64, 0, 8)[None, :]
    inside = inside * inverse[None, :]
    both = np.concatenate([np.cos(base), np.sin(base), np.cos(inside), np.sin(inside)], axis=0)
    return both.astype(np.float32)


def kernel(
    prompt, kv_down, gain, home, slot, cache, lengths, queries, news, plan, turns,
    out,
    x, w, wr, part, send_r, send_l, recv_r, recv_l,
    gain_v, turn_v, home_s, slot_s, len_s, plan_s,
    keys, q, fresh, acc, sib, piece, got,
    in_sem, ss_r, ss_l, rs_r, rs_l, ss_c, rs_c, ss_a, rs_a,
):
    f32, bf16 = jnp.float32, jnp.bfloat16
    s = lax.axis_index("section")
    c = lax.axis_index("seq")
    core = lax.rem(c, 2)
    chip = c // 2
    y, xx, z = lax.rem(chip, 4), lax.rem(chip // 4, 4), chip // 16
    right, left = (lax.rem(s + 1, 4), c), (lax.rem(s + 3, 4), c)
    sibling = (s, chip * 2 + (1 - core))

    def far_chip(i):
        return (
            lax.rem(z + i // 16, 2) * 16 + lax.rem(xx + lax.rem(i // 4, 4), 4) * 4 + lax.rem(y + lax.rem(i, 4), 4)
        )

    barrier = pltpu.get_barrier_semaphore()
    for device in (right, left, sibling):
        pl.semaphore_signal(barrier, inc=1, device_id=device, device_id_type=MESH)

    def greet(i, carry):
        pl.semaphore_signal(barrier, inc=1, device_id=(s, far_chip(i) * 2 + core), device_id_type=MESH)
        return carry

    lax.fori_loop(1, 32, greet, 0)

    loads = []

    def load(src, dst):
        copy = pltpu.make_async_copy(src, dst, in_sem.at[len(loads)])
        copy.start()
        loads.append(copy)
        return copy

    half_rows = BLK // 2
    first = [load(kv_down, w)]
    for b in range(4):
        first.append(load(prompt.at[pl.ds(b * BLK, half_rows)], x.at[0, pl.ds(b * half_rows, half_rows)]))
    small = [load(home, home_s), load(slot, slot_s), load(lengths, len_s), load(plan, plan_s)]
    second = []
    for b in range(4):
        second.append(
            load(prompt.at[pl.ds(b * BLK + half_rows, half_rows)], x.at[1, pl.ds(b * half_rows, half_rows)])
        )
    third = [
        load(cache.at[0], keys.at[pl.ds(0, CSLOT)]),
        load(cache.at[1], keys.at[pl.ds(CSLOT, CSLOT)]),
        load(news, keys.at[pl.ds(2 * CSLOT, 128)]),
        load(queries, q),
        load(gain, gain_v),
        load(turns, turn_v),
    ]

    lane8 = lax.broadcasted_iota(jnp.int32, (8, 128), 1)
    lane_low = lane8 < 64

    def project(half):
        main = jnp.dot(x[half], w[:, :LAT], preferred_element_type=f32)
        turn = jnp.dot(x[half], wr[...], preferred_element_type=f32)
        n = 4 * half_rows // ROWS
        main = main.reshape(n, 2, 8, LAT)
        turn = turn.reshape(n, 2, 8, 128)
        for h in range(2):
            for t in range(4):
                part[half * n : (half + 1) * n, h * 4 + t] = main[:, h, :, t * 128 : (t + 1) * 128]
        part[half * n : (half + 1) * n, 8] = jnp.where(lane_low[None], turn[:, 0], turn[:, 1])

    for copy in first:
        copy.wait()
    tail = w[:, LAT:]
    wr[...] = jnp.concatenate([tail, tail], axis=1)
    project(0)
    for copy in small:
        copy.wait()

    code = jnp.int32(0)
    for b in range(4):
        group = home_s[b] // 2
        code = code + lax.rem(group - s + 4, 4) * (4**b)
    base = code * TABLE

    pl.semaphore_wait(barrier, 34)

    right_copies, left_copies = [], []

    def message(m):
        word = plan_s[base + m]
        for side, (buf, got_buf, copies, ss, rs, device) in enumerate(
            (
                (send_r, recv_r, right_copies, ss_r, rs_r, right),
                (send_l, recv_l, left_copies, ss_l, rs_l, left),
            )
        ):
            field = word >> (6 * side)
            value = part[field & 31]
            if m >= LAG:
                copies[m - LAG].wait_recv()
                adds = (field >> 5) & 1
                value = value + jnp.where(adds == 1, got_buf[m - LAG], 0.0)
            buf[m] = value
            copy = pltpu.make_async_remote_copy(
                buf.at[m], got_buf.at[m], ss.at[m], rs.at[m], device_id=device, device_id_type=MESH
            )
            copy.start()
            copies.append(copy)

    for m in range(LAG):
        message(m)
    for copy in second:
        copy.wait()
    project(1)
    message(LAG)
    message(LAG + 1)
    for copy in third:
        copy.wait()

    owned = jnp.int32(0)
    slot_block = [jnp.int32(0), jnp.int32(0)]
    slot_turn = [jnp.int32(0), jnp.int32(0)]
    slot_req = [jnp.int32(-1), jnp.int32(-1)]
    written = [jnp.int32(0)] * 4
    for b in range(4):
        is_mine = home_s[b] // 2 == s
        req = lax.rem(home_s[b], 2)
        target = req * 2 + slot_s[b]
        for k in range(2):
            take = is_mine & (owned == k)
            slot_req[k] = jnp.where(take, req, slot_req[k])
            slot_turn[k] = jnp.where(take, slot_s[b], slot_turn[k])
        for t in range(4):
            written[t] = jnp.where(is_mine & (target == t), 1, written[t])
        owned = owned + jnp.where(is_mine, 1, 0)

    row = lax.broadcasted_iota(jnp.int32, (256, 1), 0)
    row_req = lax.rem(row, 8) // 4
    row_new = lax.rem(row, 2)
    row_chip = row // 8

    n_keys = 2 * CSLOT + 128
    col = lax.broadcasted_iota(jnp.int32, (1, n_keys), 1)
    cblk = col // 128
    is_written = jnp.where(cblk == 0, written[0], jnp.where(cblk == 1, written[1], jnp.where(cblk == 2, written[2], written[3])))
    length = jnp.where(col < CSLOT, len_s[0], len_s[1])
    pos = c * CSLOT + lax.rem(col, CSLOT)
    col_req = jnp.where((col < 2 * CSLOT) & (pos < length) & (is_written == 0), col // CSLOT, -1)
    own_col = col - 2 * CSLOT
    own_code = jnp.where((own_col >= 0) & (own_col < 4), own_col, -9)

    def old_part(half):
        scores = lax.dot_general(q[half, :, :576], keys[...], (((1,), (1,)), ((), ())), preferred_element_type=f32)
        scores = scores * SCALE
        here = jnp.where((half == core) & (row_chip == chip), 1, 0)
        mask = (col_req == row_req) | (
            (own_code // 2 == row_req) & (lax.rem(own_code, 2) <= row_new) & (own_code >= 0) & (here == 1)
        )
        top = jnp.max(jnp.where(mask, scores, -BIG), axis=1, keepdims=True)
        weight = jnp.where(mask, jnp.exp(scores - top), 0.0).astype(bf16)
        total = jnp.sum(weight.astype(f32), axis=1, keepdims=True)
        acc[half, :, :LAT] = jnp.dot(weight, keys[:, :LAT], preferred_element_type=f32)
        lanes = lax.broadcasted_iota(jnp.int32, (256, 128), 1)
        acc[half, :, LAT:] = jnp.where(lanes < 64, total, top)

    message(LAG + 2)
    old_part(1 - core)
    message(LAG + 3)
    old_part(core)
    for m in range(LAG + 4, MSGS):
        message(m)
    for m in range(MSGS - LAG, MSGS):
        right_copies[m].wait_recv()
        left_copies[m].wait_recv()

    sign = jnp.where(lax.rem(lane8, 64) < 32, -1.0, 1.0)
    near_half = lax.rem(lane8, 64) < 32
    gain_row = gain_v[...]
    for k in range(2):
        turn_at = c * 2 + slot_turn[k]
        cos_b = turn_v[pl.ds(turn_at, 1)]
        sin_b = turn_v[pl.ds(turn_at + 128, 1)]
        for j in range(NCH):
            word = plan_s[base + MSGS + k * NCH + j]
            value = part[word & 31] + recv_r[(word >> 5) & 31] + recv_l[(word >> 10) & 31]
            for h in range(2):
                pieces = [value[h * 4 + t] for t in range(4)]
                square = pieces[0] * pieces[0]
                for t in range(1, 4):
                    square = square + pieces[t] * pieces[t]
                factor = lax.rsqrt(jnp.sum(square, axis=1, keepdims=True) * (1.0 / LAT) + EPS)
                pieces = [p * factor * gain_row[:, t * 128 : (t + 1) * 128] for t, p in enumerate(pieces)]
                if h == 0:
                    upper = pieces
            cos_i = turn_v[256 + j * 8 : 256 + (j + 1) * 8]
            sin_i = turn_v[320 + j * 8 : 320 + (j + 1) * 8]
            cosine = cos_b * cos_i - sin_b * sin_i
            sine = (sin_b * cos_i + cos_b * sin_i) * sign
            rotary = value[8]
            swapped = jnp.where(near_half, pltpu.roll(rotary, 96, 1), pltpu.roll(rotary, 32, 1))
            turned = rotary * cosine + swapped * sine
            at = k * BLK + j * ROWS
            for t in range(4):
                fresh[at : at + ROWS, t * 128 : (t + 1) * 128] = jnp.concatenate([upper[t], pieces[t]], axis=0).astype(bf16)
            fresh[at : at + ROWS, LAT:] = jnp.concatenate(
                [jnp.where(lane_low, turned, 0.0), jnp.where(lane_low, 0.0, turned)], axis=0
            ).astype(bf16)

    fcol = lax.broadcasted_iota(jnp.int32, (1, 2 * BLK), 1)
    fresh_req = jnp.where(fcol < BLK, slot_req[0], slot_req[1])

    def new_part(half):
        scores = lax.dot_general(q[half], fresh[...], (((1,), (1,)), ((), ())), preferred_element_type=f32)
        scores = scores * SCALE
        mask = fresh_req == row_req
        old_total = acc[half, :, LAT : LAT + 1]
        old_top = acc[half, :, LAT + 64 : LAT + 65]
        top = jnp.maximum(jnp.max(jnp.where(mask, scores, -BIG), axis=1, keepdims=True), old_top)
        weight = jnp.where(mask, jnp.exp(scores - top), 0.0).astype(bf16)
        shrink = jnp.exp(old_top - top)
        total = jnp.sum(weight.astype(f32), axis=1, keepdims=True) + old_total * shrink
        acc[half, :, :LAT] = acc[half, :, :LAT] * shrink + jnp.dot(
            weight, fresh[:, :LAT], preferred_element_type=f32
        )
        lanes = lax.broadcasted_iota(jnp.int32, (256, 128), 1)
        acc[half, :, LAT:] = jnp.where(lanes < 64, total, top)

    new_part(1 - core)
    swap = pltpu.make_async_remote_copy(
        acc.at[1 - core], sib, ss_c, rs_c, device_id=sibling, device_id_type=MESH
    )
    swap.start()
    new_part(core)
    swap.wait_recv()

    mine_top = acc[core, :, LAT + 64 : LAT + 65]
    other_top = sib[:, LAT + 64 : LAT + 65]
    top = jnp.maximum(mine_top, other_top)
    fa, fb = jnp.exp(mine_top - top), jnp.exp(other_top - top)
    lanes = lax.broadcasted_iota(jnp.int32, (256, 128), 1)
    meta = jnp.where(lanes < 64, acc[core, :, LAT:] * fa + sib[:, LAT:] * fb, top)
    piece[:, :, LAT:] = meta.reshape(32, 8, 128)
    piece[:, :, :LAT] = (acc[core, :, :LAT] * fa + sib[:, :LAT] * fb).reshape(32, 8, LAT)

    def far_copy(i):
        to = far_chip(i)
        return pltpu.make_async_remote_copy(
            piece.at[to], got.at[i], ss_a.at[i], rs_a.at[i], device_id=(s, to * 2 + core), device_id_type=MESH
        )

    def far_start(i, carry):
        far_copy(i).start()
        return carry

    lax.fori_loop(1, 32, far_start, 0)
    swap.wait_send()
    for copy in right_copies + left_copies:
        copy.wait_send()

    def far_wait(i, carry):
        far_copy(i).wait()
        return carry

    lax.fori_loop(1, 32, far_wait, 0)
    got[0] = piece[chip]

    tops = [got[i, :, LAT + 64 : LAT + 65] for i in range(32)]
    top = functools.reduce(jnp.maximum, tops)
    number = jnp.zeros((8, LAT), f32)
    total = jnp.zeros((8, 1), f32)
    for i in range(32):
        factor = jnp.exp(tops[i] - top)
        number = number + got[i, :, :LAT] * factor
        total = total + got[i, :, LAT : LAT + 1] * factor
    out[...] = number / total


def body(prompt, kv_down, latent_gain, block_home, block_slot, latent_cache, cache_lengths, queries, new_rows):
    f32, bf16 = jnp.float32, jnp.bfloat16
    wide = kv_down.shape[1]
    q = queries.reshape(2, 32, 2, 4, wide).transpose(2, 1, 0, 3, 4).reshape(2, 256, wide)
    q = jnp.concatenate([q, q[..., LAT:]], axis=-1)
    news = jnp.pad(new_rows.reshape(4, wide), ((0, 124), (0, 0)))
    any_space = pl.BlockSpec(memory_space=pl.ANY)
    n_loads = 1 + 4 + 4 + 4 + 6
    dma = pltpu.SemaphoreType.DMA
    msg = (PIECE, 8, 128)
    out = pl.pallas_call(
        kernel,
        out_shape=jax.ShapeDtypeStruct((8, LAT), f32),
        in_specs=[any_space] * 11,
        out_specs=pl.BlockSpec(memory_space=pltpu.VMEM),
        scratch_shapes=[
            pltpu.VMEM((2, 256, prompt.shape[1]), bf16),
            pltpu.VMEM(kv_down.shape, bf16),
            pltpu.VMEM((kv_down.shape[0], 128), bf16),
            pltpu.VMEM((4 * NCH,) + msg, f32),
            pltpu.VMEM((MSGS,) + msg, f32),
            pltpu.VMEM((MSGS,) + msg, f32),
            pltpu.VMEM((MSGS,) + msg, f32),
            pltpu.VMEM((MSGS,) + msg, f32),
            pltpu.VMEM((1, LAT), f32),
            pltpu.VMEM((384, 128), f32),
            pltpu.SMEM((4,), jnp.int32),
            pltpu.SMEM((4,), jnp.int32),
            pltpu.SMEM((2,), jnp.int32),
            pltpu.SMEM((256 * TABLE,), jnp.int32),
            pltpu.VMEM((2 * CSLOT + 128, wide), bf16),
            pltpu.VMEM((2, 256, 640), bf16),
            pltpu.VMEM((2 * BLK, 640), bf16),
            pltpu.VMEM((2, 256, 640), f32),
            pltpu.VMEM((256, 640), f32),
            pltpu.VMEM((32, 8, 640), f32),
            pltpu.VMEM((32, 8, 640), f32),
            dma((n_loads,)),
            dma((MSGS,)),
            dma((MSGS,)),
            dma((MSGS,)),
            dma((MSGS,)),
            dma,
            dma,
            dma((32,)),
            dma((32,)),
        ],
        compiler_params=pltpu.CompilerParams(
            collective_id=0, has_side_effects=True, vmem_limit_bytes=48 * 1024 * 1024
        ),
        name="mla_decode",
    )(
        prompt, kv_down, latent_gain.reshape(1, LAT), block_home, block_slot, latent_cache, cache_lengths, q, news,
        jnp.asarray(plan_table()), jnp.asarray(turn_tables()),
    )
    return out.astype(bf16).reshape(2, 2, 2, LAT)


def solution(mesh):
    placed = (
        P("seq", "section"),
        P("section", None),
        P(),
        P("seq"),
        P("seq"),
        P("section", "seq", None),
        P("section"),
        P("section", None, None, None),
        P("section", None, None),
    )
    return jax.shard_map(body, mesh=mesh, in_specs=placed, out_specs=P("section", "seq", None, None), check_vma=False)
```

```python
import functools

import jax
import jax.numpy as jnp
import numpy as np
from jax import lax
from jax.experimental import pallas as pl
from jax.experimental.pallas import tpu as pltpu
from jax.sharding import PartitionSpec as P

MESH = pl.DeviceIdType.MESH
LAT = 512
WIDE = 576
BLK = 128
CSLOT = 256
SCALE = 192.0 ** (-0.5)
EPS = 1e-6
BIG = 1e30

ROWS = 16
NCH = BLK // ROWS
LAG = 8
EXTRA = 4
MSGS = 2 * NCH + EXTRA
PIECE = 9
SPLITS = ((0, PIECE),)
TABLE = 128


def chunk_id(block, chunk):
    half = NCH // 2
    return (chunk // half) * (4 * half) + block * half + chunk % half


def passes(rel):
    n_right, n_left = rel.count(1), rel.count(3)
    opposite = [b for b in range(4) if rel[b] == 2]
    if len(opposite) == 1:
        right = 1 if n_right <= n_left else 0
    else:
        right = 1 + (n_left == 2) - (n_right == 2)
    right = min(max(right, 0), len(opposite))
    items = [(b, j) for j in range(NCH) for b in opposite]
    if len(opposite) == 2 and right == 2:
        return items[EXTRA:], items[:EXTRA]
    if len(opposite) == 2 and right == 0:
        return items[:EXTRA], items[EXTRA:]
    return [v for v in items if v[0] in opposite[:right]], [v for v in items if v[0] in opposite[right:]]


def lane_plan(rel, side):
    near, step = (1, 1) if side == 0 else (3, -1)
    mine = passes(rel)[side]
    behind = passes([(r + step) % 4 for r in rel])[side]
    spots = {i: v + (0,) for i, v in enumerate(mine)}
    for i, v in enumerate(behind):
        assert i + LAG not in spots
        spots[i + LAG] = v + (1,)
    plain = [(b, j) for j in range(NCH) for b in range(4) if rel[b] == near and (b, j) not in behind]
    free = [m for m in range(MSGS) if m not in spots]
    spots.update({m: v + (0,) for m, v in zip(free, plain)})
    return spots


@functools.lru_cache(None)
def plan_table():
    table = np.zeros((256, TABLE), np.int32)
    for code in range(256):
        rel = [(code >> (2 * b)) & 3 for b in range(4)]
        if max(rel.count(g) for g in range(4)) > 2:
            continue
        for side in range(2):
            for m, (b, j, adds) in lane_plan(rel, side).items():
                table[code, m] |= (chunk_id(b, j) | (adds << 5)) << (6 * side)
        owned = [b for b in range(4) if rel[b] == 0]
        from_left = lane_plan([(r + 1) % 4 for r in rel], 0)
        from_right = lane_plan([(r - 1) % 4 for r in rel], 1)
        for k, b in enumerate(owned):
            for j in range(NCH):
                at_left = [m for m, v in from_left.items() if v[:2] == (b, j)][0]
                at_right = [m for m, v in from_right.items() if v[:2] == (b, j)][0]
                table[code, MSGS + k * NCH + j] = chunk_id(b, j) | (at_left << 5) | (at_right << 10)
    return table


@functools.lru_cache(None)
def turn_tables():
    lane = np.arange(128)
    inverse = 10000.0 ** (-2.0 * (lane % 32) / 64.0)
    base = (np.arange(128) * 128.0)[:, None] * inverse[None, :]
    row = np.arange(8 * NCH)
    inside = ((row // 8) * 16 + row % 8)[:, None] + np.where(lane < 64, 0, 8)[None, :]
    inside = inside * inverse[None, :]
    both = np.concatenate([np.cos(base), np.sin(base), np.cos(inside), np.sin(inside)], axis=0)
    return both.astype(np.float32)


def kernel(
    prompt, kv_down, gain, home, slot, cache, lengths, queries, news, plan, turns,
    out,
    x, w, part, send_r, send_l, recv_r, recv_l,
    gain_v, turn_v, home_s, slot_s, len_s, plan_v, row_v, plan_s,
    keys, qt, q, news_v, news_f, fresh, acc, sib, piece, got,
    in_sem, ss_r, ss_l, rs_r, rs_l, ss_c, rs_c, ss_a, rs_a,
):
    f32, bf16 = jnp.float32, jnp.bfloat16
    s = lax.axis_index("section")
    c = lax.axis_index("seq")
    core = lax.rem(c, 2)
    chip = c // 2
    y, xx, z = lax.rem(chip, 4), lax.rem(chip // 4, 4), chip // 16
    right, left = (lax.rem(s + 1, 4), c), (lax.rem(s + 3, 4), c)
    sibling = (s, chip * 2 + (1 - core))

    def far_chip(i):
        return (
            lax.rem(z + i // 16, 2) * 16 + lax.rem(xx + lax.rem(i // 4, 4), 4) * 4 + lax.rem(y + lax.rem(i, 4), 4)
        )

    loads = []

    def load(src, dst):
        copy = pltpu.make_async_copy(src, dst, in_sem.at[len(loads)])
        copy.start()
        loads.append(copy)
        return copy

    small = [load(home, home_s), load(slot, slot_s), load(lengths, len_s), load(plan, plan_v)]
    half_rows = BLK // 2
    first = [load(kv_down, w.at[pl.ds(0, WIDE)]), load(kv_down.at[pl.ds(LAT, 64)], w.at[pl.ds(WIDE, 64)])]
    for b in range(4):
        first.append(load(prompt.at[pl.ds(b * BLK, half_rows)], x.at[0, pl.ds(b * half_rows, half_rows)]))
    barrier = pltpu.get_barrier_semaphore()
    for device in (right, left, sibling):
        pl.semaphore_signal(barrier, inc=1, device_id=device, device_id_type=MESH)

    def greet(i, carry):
        pl.semaphore_signal(barrier, inc=1, device_id=(s, far_chip(i) * 2 + core), device_id_type=MESH)
        return carry

    lax.fori_loop(1, 32, greet, 0)

    second = []
    for b in range(4):
        second.append(
            load(prompt.at[pl.ds(b * BLK + half_rows, half_rows)], x.at[1, pl.ds(b * half_rows, half_rows)])
        )
    third = [load(cache, keys), load(news, news_v), load(gain, gain_v), load(turns, turn_v)]
    for r in range(2):
        for n in range(2):
            third.append(load(queries.at[r, n], qt.at[r, n, pl.ds(0, WIDE)]))
            third.append(load(queries.at[r, n, pl.ds(LAT, 64)], qt.at[r, n, pl.ds(WIDE, 64)]))

    lane8 = lax.broadcasted_iota(jnp.int32, (8, 128), 1)
    lane_low = lane8 < 64

    def dot_t(a, b):
        return lax.dot_general(a, b, (((1,), (1,)), ((), ())), preferred_element_type=f32)

    def project(half):
        both = dot_t(x[half], w[...])
        main, turn = both[:, :LAT], both[:, LAT:]
        n = 4 * half_rows // ROWS
        main = main.reshape(n, 2, 8, LAT)
        turn = turn.reshape(n, 2, 8, 128)
        for h in range(2):
            for t in range(4):
                part[half * n : (half + 1) * n, h * 5 + t] = main[:, h, :, t * 128 : (t + 1) * 128]
        part[half * n : (half + 1) * n, 4] = jnp.where(lane_low[None], turn[:, 0], turn[:, 1])

    for copy in small:
        copy.wait()
    code = jnp.int32(0)
    for b in range(4):
        group = home_s[b] // 2
        code = code + lax.rem(group - s + 4, 4) * (4**b)
    row_v[...] = plan_v[pl.ds(code, 1)]
    row_copy = load(row_v, plan_s)

    for copy in first:
        copy.wait()
    project(0)
    row_copy.wait()
    pl.semaphore_wait(barrier, 34)

    right_copies, left_copies = [], []

    def message(m):
        word = plan_s[0, m]
        for part_at, tiles in SPLITS:
            for side, (buf, got_buf, copies, ss, rs, device) in enumerate(
                (
                    (send_r, recv_r, right_copies, ss_r, rs_r, right),
                    (send_l, recv_l, left_copies, ss_l, rs_l, left),
                )
            ):
                field = word >> (6 * side)
                value = part[field & 31, pl.ds(part_at, tiles)]
                at = len(copies)
                if m >= LAG:
                    copies[at - LAG * len(SPLITS)].wait_recv()
                    adds = (field >> 5) & 1
                    value = value + jnp.where(adds == 1, got_buf[m - LAG, pl.ds(part_at, tiles)], 0.0)
                buf[m, pl.ds(part_at, tiles)] = value
                copy = pltpu.make_async_remote_copy(
                    buf.at[m, pl.ds(part_at, tiles)],
                    got_buf.at[m, pl.ds(part_at, tiles)],
                    ss.at[at],
                    rs.at[at],
                    device_id=device,
                    device_id_type=MESH,
                )
                copy.start()
                copies.append(copy)

    for m in range(NCH // 2):
        message(m)
    for copy in second:
        copy.wait()
    project(1)
    for m in range(NCH // 2, LAG):
        message(m)
    for copy in third:
        copy.wait()

    owned = jnp.int32(0)
    slot_block = [jnp.int32(0), jnp.int32(0)]
    slot_turn = [jnp.int32(0), jnp.int32(0)]
    slot_req = [jnp.int32(-1), jnp.int32(-1)]
    written = [jnp.int32(0)] * 4
    for b in range(4):
        is_mine = home_s[b] // 2 == s
        req = lax.rem(home_s[b], 2)
        target = req * 2 + slot_s[b]
        for k in range(2):
            take = is_mine & (owned == k)
            slot_req[k] = jnp.where(take, req, slot_req[k])
            slot_turn[k] = jnp.where(take, slot_s[b], slot_turn[k])
        for t in range(4):
            written[t] = jnp.where(is_mine & (target == t), 1, written[t])
        owned = owned + jnp.where(is_mine, 1, 0)

    row = lax.broadcasted_iota(jnp.int32, (256, 1), 0)
    row_req = lax.rem(row, 8) // 4
    row_new = lax.rem(row, 2)
    row_chip = row // 8

    n_keys = 2 * CSLOT + 128
    col = lax.broadcasted_iota(jnp.int32, (1, n_keys), 1)
    cblk = col // 128
    is_written = jnp.where(cblk == 0, written[0], jnp.where(cblk == 1, written[1], jnp.where(cblk == 2, written[2], written[3])))
    length = jnp.where(col < CSLOT, len_s[0], len_s[1])
    pos = c * CSLOT + lax.rem(col, CSLOT)
    col_req = jnp.where((col < 2 * CSLOT) & (pos < length) & (is_written == 0), col // CSLOT, -1)
    own_col = col - 2 * CSLOT
    own_code = jnp.where((own_col >= 0) & (own_col < 4), own_col, -9)

    def order_queries(half):
        i = lax.broadcasted_iota(jnp.int32, (256, 1), 0)
        head = (i // 8) * 4 + half * 2 + lax.rem(i // 2, 2)
        pick = lax.broadcasted_iota(jnp.int32, (256, 128), 1)
        rows = jnp.zeros((256, 640), f32)
        for r in range(2):
            for n in range(2):
                wanted = jnp.where((lax.rem(i // 4, 2) == r) & (lax.rem(i, 2) == n), head, -1)
                rows = rows + dot_t(jnp.where(pick == wanted, 1.0, 0.0).astype(bf16), qt[r, n])
        q[half] = rows.astype(bf16)

    def old_part(half):
        rows = q[half, :, :WIDE]
        scores = jnp.concatenate(
            [
                jnp.dot(rows, keys[0], preferred_element_type=f32),
                jnp.dot(rows, keys[1], preferred_element_type=f32),
                dot_t(rows, news_f[...].astype(bf16)),
            ],
            axis=1,
        )
        scores = scores * SCALE
        here = jnp.where((half == core) & (row_chip == chip), 1, 0)
        mask = (col_req == row_req) | (
            (own_code // 2 == row_req) & (lax.rem(own_code, 2) <= row_new) & (own_code >= 0) & (here == 1)
        )
        top = jnp.max(jnp.where(mask, scores, -BIG), axis=1, keepdims=True)
        weight = jnp.where(mask, jnp.exp(scores - top), 0.0).astype(bf16)
        total = jnp.sum(weight.astype(f32), axis=1, keepdims=True)
        acc[half, :, :LAT] = (
            dot_t(weight[:, :CSLOT], keys[0, :LAT])
            + dot_t(weight[:, CSLOT : 2 * CSLOT], keys[1, :LAT])
            + jnp.dot(weight[:, 2 * CSLOT :], news_f[:, :LAT].astype(bf16), preferred_element_type=f32)
        )
        lanes = lax.broadcasted_iota(jnp.int32, (256, 128), 1)
        acc[half, :, LAT:] = jnp.where(lanes < 64, total, top)

    news_f[...] = jnp.zeros_like(news_f)
    for r in range(2):
        news_f[2 * r : 2 * r + 2] = news_v[r].astype(f32)
    order_queries(1 - core)
    order_queries(core)
    message(LAG)
    message(LAG + 1)
    old_part(1 - core)
    message(LAG + 2)
    old_part(core)
    for m in range(LAG + 3, MSGS):
        message(m)
    for at in range((MSGS - LAG) * len(SPLITS), MSGS * len(SPLITS)):
        right_copies[at].wait_recv()
        left_copies[at].wait_recv()

    sign = jnp.where(lax.rem(lane8, 64) < 32, -1.0, 1.0)
    near_half = lax.rem(lane8, 64) < 32
    gain_row = gain_v[...]
    for k in range(2):
        turn_at = c * 2 + slot_turn[k]
        cos_b = turn_v[pl.ds(turn_at, 1)]
        sin_b = turn_v[pl.ds(turn_at + 128, 1)]
        for j in range(NCH):
            word = plan_s[0, MSGS + k * NCH + j]
            value = part[word & 31] + recv_r[(word >> 5) & 31] + recv_l[(word >> 10) & 31]
            for h in range(2):
                pieces = [value[h * 5 + t] for t in range(4)]
                square = pieces[0] * pieces[0]
                for t in range(1, 4):
                    square = square + pieces[t] * pieces[t]
                factor = lax.rsqrt(jnp.sum(square, axis=1, keepdims=True) * (1.0 / LAT) + EPS)
                pieces = [p * factor * gain_row[:, t * 128 : (t + 1) * 128] for t, p in enumerate(pieces)]
                if h == 0:
                    upper = pieces
            cos_i = turn_v[256 + j * 8 : 256 + (j + 1) * 8]
            sin_i = turn_v[320 + j * 8 : 320 + (j + 1) * 8]
            cosine = cos_b * cos_i - sin_b * sin_i
            sine = (sin_b * cos_i + cos_b * sin_i) * sign
            rotary = value[4]
            swapped = jnp.where(near_half, pltpu.roll(rotary, 96, 1), pltpu.roll(rotary, 32, 1))
            turned = rotary * cosine + swapped * sine
            at = k * BLK + j * ROWS
            for t in range(4):
                fresh[at : at + ROWS, t * 128 : (t + 1) * 128] = jnp.concatenate([upper[t], pieces[t]], axis=0).astype(bf16)
            fresh[at : at + ROWS, LAT:] = jnp.concatenate(
                [jnp.where(lane_low, turned, 0.0), jnp.where(lane_low, 0.0, turned)], axis=0
            ).astype(bf16)

    fcol = lax.broadcasted_iota(jnp.int32, (1, 2 * BLK), 1)
    fresh_req = jnp.where(fcol < BLK, slot_req[0], slot_req[1])

    def new_part(half):
        scores = lax.dot_general(q[half], fresh[...], (((1,), (1,)), ((), ())), preferred_element_type=f32)
        scores = scores * SCALE
        mask = fresh_req == row_req
        old_total = acc[half, :, LAT : LAT + 1]
        old_top = acc[half, :, LAT + 64 : LAT + 65]
        top = jnp.maximum(jnp.max(jnp.where(mask, scores, -BIG), axis=1, keepdims=True), old_top)
        weight = jnp.where(mask, jnp.exp(scores - top), 0.0).astype(bf16)
        shrink = jnp.exp(old_top - top)
        total = jnp.sum(weight.astype(f32), axis=1, keepdims=True) + old_total * shrink
        acc[half, :, :LAT] = acc[half, :, :LAT] * shrink + jnp.dot(
            weight, fresh[:, :LAT], preferred_element_type=f32
        )
        lanes = lax.broadcasted_iota(jnp.int32, (256, 128), 1)
        acc[half, :, LAT:] = jnp.where(lanes < 64, total, top)

    new_part(1 - core)
    swap = pltpu.make_async_remote_copy(
        acc.at[1 - core], sib, ss_c, rs_c, device_id=sibling, device_id_type=MESH
    )
    swap.start()
    new_part(core)
    swap.wait_recv()

    mine_top = acc[core, :, LAT + 64 : LAT + 65]
    other_top = sib[:, LAT + 64 : LAT + 65]
    top = jnp.maximum(mine_top, other_top)
    fa, fb = jnp.exp(mine_top - top), jnp.exp(other_top - top)
    lanes = lax.broadcasted_iota(jnp.int32, (256, 128), 1)
    meta = jnp.where(lanes < 64, acc[core, :, LAT:] * fa + sib[:, LAT:] * fb, top)
    piece[:, :, LAT:] = meta.reshape(32, 8, 128)
    piece[:, :, :LAT] = (acc[core, :, :LAT] * fa + sib[:, :LAT] * fb).reshape(32, 8, LAT)

    def far_copy(i):
        to = far_chip(i)
        return pltpu.make_async_remote_copy(
            piece.at[to], got.at[i], ss_a.at[i], rs_a.at[i], device_id=(s, to * 2 + core), device_id_type=MESH
        )

    def far_start(i, carry):
        far_copy(i).start()
        return carry

    lax.fori_loop(1, 32, far_start, 0)
    swap.wait_send()
    for copy in right_copies + left_copies:
        copy.wait_send()

    def far_wait(i, carry):
        far_copy(i).wait()
        return carry

    lax.fori_loop(1, 32, far_wait, 0)
    got[0] = piece[chip]

    tops = [got[i, :, LAT + 64 : LAT + 65] for i in range(32)]
    top = functools.reduce(jnp.maximum, tops)
    number = jnp.zeros((8, LAT), f32)
    total = jnp.zeros((8, 1), f32)
    for i in range(32):
        factor = jnp.exp(tops[i] - top)
        number = number + got[i, :, :LAT] * factor
        total = total + got[i, :, LAT : LAT + 1] * factor
    out[...] = (number / total).astype(bf16)


def body(prompt, kv_down, latent_gain, block_home, block_slot, latent_cache, cache_lengths, queries, new_rows):
    f32, bf16 = jnp.float32, jnp.bfloat16
    any_space = pl.BlockSpec(memory_space=pl.ANY)
    n_loads = 3 + 4 + 4 + 4 + 12
    dma = pltpu.SemaphoreType.DMA
    msg = (PIECE, 8, 128)
    out = pl.pallas_call(
        kernel,
        out_shape=jax.ShapeDtypeStruct((8, LAT), bf16),
        in_specs=[any_space] * 11,
        out_specs=pl.BlockSpec(memory_space=pltpu.VMEM),
        scratch_shapes=[
            pltpu.VMEM((2, 256, prompt.shape[1]), bf16),
            pltpu.VMEM((640, kv_down.shape[0]), bf16),
            pltpu.VMEM((4 * NCH,) + msg, f32),
            pltpu.VMEM((MSGS,) + msg, f32),
            pltpu.VMEM((MSGS,) + msg, f32),
            pltpu.VMEM((MSGS,) + msg, f32),
            pltpu.VMEM((MSGS,) + msg, f32),
            pltpu.VMEM((1, LAT), f32),
            pltpu.VMEM((384, 128), f32),
            pltpu.SMEM((4,), jnp.int32),
            pltpu.SMEM((4,), jnp.int32),
            pltpu.SMEM((2,), jnp.int32),
            pltpu.VMEM((256, TABLE), jnp.int32),
            pltpu.VMEM((1, TABLE), jnp.int32),
            pltpu.SMEM((1, TABLE), jnp.int32),
            pltpu.VMEM((2, WIDE, CSLOT), bf16),
            pltpu.VMEM((2, 2, 640, 128), bf16),
            pltpu.VMEM((2, 256, 640), bf16),
            pltpu.VMEM((2, 2, WIDE), bf16),
            pltpu.VMEM((128, WIDE), f32),
            pltpu.VMEM((2 * BLK, 640), bf16),
            pltpu.VMEM((2, 256, 640), f32),
            pltpu.VMEM((256, 640), f32),
            pltpu.VMEM((32, 8, 640), f32),
            pltpu.VMEM((32, 8, 640), f32),
            dma((n_loads,)),
            dma((MSGS * len(SPLITS),)),
            dma((MSGS * len(SPLITS),)),
            dma((MSGS * len(SPLITS),)),
            dma((MSGS * len(SPLITS),)),
            dma,
            dma,
            dma((32,)),
            dma((32,)),
        ],
        compiler_params=pltpu.CompilerParams(
            collective_id=0, has_side_effects=True, vmem_limit_bytes=62 * 1024 * 1024
        ),
        name="mla_decode",
    )(
        prompt, kv_down.T, latent_gain.reshape(1, LAT), block_home, block_slot, latent_cache.transpose(0, 2, 1),
        cache_lengths, queries.transpose(0, 2, 3, 1), new_rows,
        jnp.asarray(plan_table()), jnp.asarray(turn_tables()),
    )
    return out.reshape(2, 2, 2, LAT)


def solution(mesh):
    placed = (
        P("seq", "section"),
        P("section", None),
        P(),
        P("seq"),
        P("seq"),
        P("section", "seq", None),
        P("section"),
        P("section", None, None, None),
        P("section", None, None),
    )
    return jax.shard_map(body, mesh=mesh, in_specs=placed, out_specs=P("section", "seq", None, None), check_vma=False)
```

```python
import functools

import jax
import jax.numpy as jnp
import numpy as np
from jax import lax
from jax.experimental import pallas as pl
from jax.experimental.pallas import tpu as pltpu
from jax.sharding import PartitionSpec as P

MESH = pl.DeviceIdType.MESH
LAT = 512
WIDE = 576
BLK = 128
CSLOT = 256
SCALE = 192.0 ** (-0.5)
EPS = 1e-6
BIG = 1e30

ROWS = 16
NCH = BLK // ROWS
LAG = 8
SHORT = 4
EXTRA = 2
MSGS = 2 * NCH + EXTRA
PIECE = 9
SPLITS = ((0, PIECE),)
TABLE = 128


def chunk_id(block, chunk):
    half = NCH // 2
    return (chunk // half) * (4 * half) + block * half + chunk % half


def passes(rel):
    n_right, n_left = rel.count(1), rel.count(3)
    opposite = [b for b in range(4) if rel[b] == 2]
    if len(opposite) == 1:
        right = 1 if n_right <= n_left else 0
    else:
        right = 1 + (n_left == 2) - (n_right == 2)
    right = min(max(right, 0), len(opposite))
    items = [(b, j) for j in range(NCH) for b in opposite]
    if len(opposite) == 2 and right == 2:
        return items[EXTRA:], items[:EXTRA]
    if len(opposite) == 2 and right == 0:
        return items[:EXTRA], items[EXTRA:]
    return [v for v in items if v[0] in opposite[:right]], [v for v in items if v[0] in opposite[right:]]


def lane_plan(rel, side):
    near, step = (1, 1) if side == 0 else (3, -1)
    mine = passes(rel)[side]
    behind = passes([(r + step) % 4 for r in rel])[side]
    spots = {i: v + (0,) for i, v in enumerate(mine)}
    many = len(behind) > LAG
    for i, v in enumerate(behind):
        at = i + (SHORT if many else LAG)
        spots[at] = v + (2 if many else 1,)
    plain = [(b, j) for j in range(NCH) for b in range(4) if rel[b] == near and (b, j) not in behind]
    free = [m for m in range(MSGS) if m not in spots]
    spots.update({m: v + (0,) for m, v in zip(free, plain)})
    return spots


@functools.lru_cache(None)
def plan_table():
    table = np.zeros((256, TABLE), np.int32)
    for code in range(256):
        rel = [(code >> (2 * b)) & 3 for b in range(4)]
        if max(rel.count(g) for g in range(4)) > 2:
            continue
        for side in range(2):
            for m, (b, j, adds) in lane_plan(rel, side).items():
                table[code, m] |= (chunk_id(b, j) | (adds << 5)) << (7 * side)
        owned = [b for b in range(4) if rel[b] == 0]
        from_left = lane_plan([(r + 1) % 4 for r in rel], 0)
        from_right = lane_plan([(r - 1) % 4 for r in rel], 1)
        for k, b in enumerate(owned):
            for j in range(NCH):
                at_left = [m for m, v in from_left.items() if v[:2] == (b, j)][0]
                at_right = [m for m, v in from_right.items() if v[:2] == (b, j)][0]
                table[code, MSGS + k * NCH + j] = chunk_id(b, j) | (at_left << 5) | (at_right << 10)
    return table


@functools.lru_cache(None)
def turn_tables():
    lane = np.arange(128)
    inverse = 10000.0 ** (-2.0 * (lane % 32) / 64.0)
    base = (np.arange(128) * 128.0)[:, None] * inverse[None, :]
    row = np.arange(8 * NCH)
    inside = ((row // 8) * 16 + row % 8)[:, None] + np.where(lane < 64, 0, 8)[None, :]
    inside = inside * inverse[None, :]
    both = np.concatenate([np.cos(base), np.sin(base), np.cos(inside), np.sin(inside)], axis=0)
    return both.astype(np.float32)


def kernel(
    prompt, kv_down, gain, home, slot, cache, lengths, queries, news, plan, turns,
    out,
    x, w, part, send_r, send_l, recv_r, recv_l,
    gain_v, turn_v, home_s, slot_s, len_s, plan_v, row_v, plan_s,
    keys, qt, q, news_v, news_f, fresh, acc, sib, piece, got,
    in_sem, ss_r, ss_l, rs_r, rs_l, ss_c, rs_c, ss_a, rs_a,
):
    f32, bf16 = jnp.float32, jnp.bfloat16
    s = lax.axis_index("section")
    c = lax.axis_index("seq")
    core = lax.rem(c, 2)
    chip = c // 2
    y, xx, z = lax.rem(chip, 4), lax.rem(chip // 4, 4), chip // 16
    right, left = (lax.rem(s + 1, 4), c), (lax.rem(s + 3, 4), c)
    sibling = (s, chip * 2 + (1 - core))

    def far_chip(i):
        return (
            lax.rem(z + i // 16, 2) * 16 + lax.rem(xx + lax.rem(i // 4, 4), 4) * 4 + lax.rem(y + lax.rem(i, 4), 4)
        )

    loads = []

    def load(src, dst):
        copy = pltpu.make_async_copy(src, dst, in_sem.at[len(loads)])
        copy.start()
        loads.append(copy)
        return copy

    first = [
        load(kv_down, w.at[pl.ds(0, WIDE)]),
        load(prompt.at[:, 0], x.at[0]),
        load(kv_down.at[pl.ds(LAT, 64)], w.at[pl.ds(WIDE, 64)]),
    ]
    small = [load(home, home_s), load(plan, plan_v)]
    barrier = pltpu.get_barrier_semaphore()
    for device in (right, left, sibling):
        pl.semaphore_signal(barrier, inc=1, device_id=device, device_id_type=MESH)

    def greet(i, carry):
        pl.semaphore_signal(barrier, inc=1, device_id=(s, far_chip(i) * 2 + core), device_id_type=MESH)
        return carry

    lax.fori_loop(1, 32, greet, 0)

    second = [load(prompt.at[:, 1], x.at[1])]

    lane8 = lax.broadcasted_iota(jnp.int32, (8, 128), 1)
    lane_low = lane8 < 64

    def dot_t(a, b):
        return lax.dot_general(a, b, (((1,), (1,)), ((), ())), preferred_element_type=f32)

    def project(half):
        both = dot_t(x[half].reshape(256, x.shape[3]), w[...])
        main, turn = both[:, :LAT], both[:, LAT:]
        n = 4 * (BLK // 2) // ROWS
        main = main.reshape(n, 2, 8, LAT)
        turn = turn.reshape(n, 2, 8, 128)
        for h in range(2):
            for t in range(4):
                part[half * n : (half + 1) * n, h * 5 + t] = main[:, h, :, t * 128 : (t + 1) * 128]
        part[half * n : (half + 1) * n, 4] = jnp.where(lane_low[None], turn[:, 0], turn[:, 1])

    for copy in small:
        copy.wait()
    code = jnp.int32(0)
    for b in range(4):
        group = home_s[b] // 2
        code = code + lax.rem(group - s + 4, 4) * (4**b)
    row_v[...] = plan_v[pl.ds(code, 1)]
    row_copy = load(row_v, plan_s)

    third = [
        load(slot, slot_s),
        load(lengths, len_s),
        load(cache, keys),
        load(news, news_v),
        load(gain, gain_v),
        load(turns, turn_v),
        load(queries, qt.at[:, :, pl.ds(0, WIDE)]),
        load(queries.at[:, :, pl.ds(LAT, 64)], qt.at[:, :, pl.ds(WIDE, 64)]),
    ]
    for copy in first:
        copy.wait()
    project(0)
    row_copy.wait()
    pl.semaphore_wait(barrier, 34)

    right_copies, left_copies = [], []

    def message(m):
        word = plan_s[0, m]
        for part_at, tiles in SPLITS:
            for side, (buf, got_buf, copies, ss, rs, device) in enumerate(
                (
                    (send_r, recv_r, right_copies, ss_r, rs_r, right),
                    (send_l, recv_l, left_copies, ss_l, rs_l, left),
                )
            ):
                field = word >> (7 * side)
                value = part[field & 31, pl.ds(part_at, tiles)]
                at = len(copies)
                adds = (field >> 5) & 3
                if m >= SHORT:
                    copies[m - SHORT].wait_recv()
                    value = value + jnp.where(adds == 2, got_buf[m - SHORT], 0.0)
                if m >= LAG:
                    value = value + jnp.where(adds == 1, got_buf[m - LAG], 0.0)
                buf[m, pl.ds(part_at, tiles)] = value
                copy = pltpu.make_async_remote_copy(
                    buf.at[m, pl.ds(part_at, tiles)],
                    got_buf.at[m, pl.ds(part_at, tiles)],
                    ss.at[at],
                    rs.at[at],
                    device_id=device,
                    device_id_type=MESH,
                )
                copy.start()
                copies.append(copy)

    for m in range(NCH // 2):
        message(m)
    for copy in second:
        copy.wait()
    project(1)
    for m in range(NCH // 2, LAG):
        message(m)
    for copy in third:
        copy.wait()

    owned = jnp.int32(0)
    slot_block = [jnp.int32(0), jnp.int32(0)]
    slot_turn = [jnp.int32(0), jnp.int32(0)]
    slot_req = [jnp.int32(-1), jnp.int32(-1)]
    written = [jnp.int32(0)] * 4
    for b in range(4):
        is_mine = home_s[b] // 2 == s
        req = lax.rem(home_s[b], 2)
        target = req * 2 + slot_s[b]
        for k in range(2):
            take = is_mine & (owned == k)
            slot_req[k] = jnp.where(take, req, slot_req[k])
            slot_turn[k] = jnp.where(take, slot_s[b], slot_turn[k])
        for t in range(4):
            written[t] = jnp.where(is_mine & (target == t), 1, written[t])
        owned = owned + jnp.where(is_mine, 1, 0)

    row = lax.broadcasted_iota(jnp.int32, (256, 1), 0)
    row_req = lax.rem(row, 8) // 4
    row_new = lax.rem(row, 2)
    row_chip = row // 8

    n_keys = 2 * CSLOT + 128
    col = lax.broadcasted_iota(jnp.int32, (1, n_keys), 1)
    cblk = col // 128
    is_written = jnp.where(cblk == 0, written[0], jnp.where(cblk == 1, written[1], jnp.where(cblk == 2, written[2], written[3])))
    length = jnp.where(col < CSLOT, len_s[0], len_s[1])
    pos = c * CSLOT + lax.rem(col, CSLOT)
    col_req = jnp.where((col < 2 * CSLOT) & (pos < length) & (is_written == 0), col // CSLOT, -1)
    own_col = col - 2 * CSLOT
    own_code = jnp.where((own_col >= 0) & (own_col < 4), own_col, -9)

    def order_queries(half):
        i = lax.broadcasted_iota(jnp.int32, (256, 1), 0)
        head = (i // 8) * 4 + half * 2 + lax.rem(i // 2, 2)
        pick = lax.broadcasted_iota(jnp.int32, (256, 128), 1)
        rows = jnp.zeros((256, 640), f32)
        for r in range(2):
            for n in range(2):
                wanted = jnp.where((lax.rem(i // 4, 2) == r) & (lax.rem(i, 2) == n), head, -1)
                rows = rows + dot_t(jnp.where(pick == wanted, 1.0, 0.0).astype(bf16), qt[r, n])
        q[half] = rows.astype(bf16)

    def old_part(half):
        rows = q[half, :, :WIDE]
        scores = jnp.concatenate(
            [
                jnp.dot(rows, keys[0], preferred_element_type=f32),
                jnp.dot(rows, keys[1], preferred_element_type=f32),
                dot_t(rows, news_f[...].astype(bf16)),
            ],
            axis=1,
        )
        scores = scores * SCALE
        here = jnp.where((half == core) & (row_chip == chip), 1, 0)
        mask = (col_req == row_req) | (
            (own_code // 2 == row_req) & (lax.rem(own_code, 2) <= row_new) & (own_code >= 0) & (here == 1)
        )
        top = jnp.max(jnp.where(mask, scores, -BIG), axis=1, keepdims=True)
        weight = jnp.where(mask, jnp.exp(scores - top), 0.0).astype(bf16)
        total = jnp.sum(weight.astype(f32), axis=1, keepdims=True)
        acc[half, :, :LAT] = (
            dot_t(weight[:, :CSLOT], keys[0, :LAT])
            + dot_t(weight[:, CSLOT : 2 * CSLOT], keys[1, :LAT])
            + jnp.dot(weight[:, 2 * CSLOT :], news_f[:, :LAT].astype(bf16), preferred_element_type=f32)
        )
        acc[half, :, LAT : LAT + 128] = jnp.broadcast_to(total, (256, 128))
        acc[half, :, LAT + 128 :] = jnp.broadcast_to(top, (256, 128))

    news_f[...] = jnp.zeros_like(news_f)
    for r in range(2):
        news_f[2 * r : 2 * r + 2] = news_v[r].astype(f32)
    order_queries(1 - core)
    order_queries(core)
    message(LAG)
    message(LAG + 1)
    old_part(1 - core)
    message(LAG + 2)
    old_part(core)
    for m in range(LAG + 3, MSGS):
        message(m)
    for at in range(MSGS - SHORT, MSGS):
        right_copies[at].wait_recv()
        left_copies[at].wait_recv()

    sign = jnp.where(lax.rem(lane8, 64) < 32, -1.0, 1.0)
    near_half = lax.rem(lane8, 64) < 32
    gain_row = gain_v[...]
    for k in range(2):
        turn_at = c * 2 + slot_turn[k]
        cos_b = turn_v[pl.ds(turn_at, 1)]
        sin_b = turn_v[pl.ds(turn_at + 128, 1)]
        for j in range(NCH):
            word = plan_s[0, MSGS + k * NCH + j]
            value = part[word & 31] + recv_r[(word >> 5) & 31] + recv_l[(word >> 10) & 31]
            for h in range(2):
                pieces = [value[h * 5 + t] for t in range(4)]
                square = pieces[0] * pieces[0]
                for t in range(1, 4):
                    square = square + pieces[t] * pieces[t]
                factor = lax.rsqrt(jnp.sum(square, axis=1, keepdims=True) * (1.0 / LAT) + EPS)
                pieces = [p * factor * gain_row[:, t * 128 : (t + 1) * 128] for t, p in enumerate(pieces)]
                if h == 0:
                    upper = pieces
            cos_i = turn_v[256 + j * 8 : 256 + (j + 1) * 8]
            sin_i = turn_v[320 + j * 8 : 320 + (j + 1) * 8]
            cosine = cos_b * cos_i - sin_b * sin_i
            sine = (sin_b * cos_i + cos_b * sin_i) * sign
            rotary = value[4]
            swapped = jnp.where(near_half, pltpu.roll(rotary, 96, 1), pltpu.roll(rotary, 32, 1))
            turned = rotary * cosine + swapped * sine
            at = k * BLK + j * ROWS
            for t in range(4):
                fresh[at : at + ROWS, t * 128 : (t + 1) * 128] = jnp.concatenate([upper[t], pieces[t]], axis=0).astype(bf16)
            fresh[at : at + ROWS, LAT:] = jnp.concatenate(
                [jnp.where(lane_low, turned, 0.0), jnp.where(lane_low, 0.0, turned)], axis=0
            ).astype(bf16)

    fcol = lax.broadcasted_iota(jnp.int32, (1, 2 * BLK), 1)
    fresh_req = jnp.where(fcol < BLK, slot_req[0], slot_req[1])

    def new_part(half):
        scores = lax.dot_general(q[half], fresh[...], (((1,), (1,)), ((), ())), preferred_element_type=f32)
        scores = scores * SCALE
        mask = fresh_req == row_req
        old_total = acc[half, :, LAT : LAT + 1]
        old_top = acc[half, :, LAT + 128 : LAT + 129]
        top = jnp.maximum(jnp.max(jnp.where(mask, scores, -BIG), axis=1, keepdims=True), old_top)
        weight = jnp.where(mask, jnp.exp(scores - top), 0.0).astype(bf16)
        shrink = jnp.exp(old_top - top)
        total = jnp.sum(weight.astype(f32), axis=1, keepdims=True) + old_total * shrink
        acc[half, :, :LAT] = acc[half, :, :LAT] * shrink + jnp.dot(
            weight, fresh[:, :LAT], preferred_element_type=f32
        )
        acc[half, :, LAT : LAT + 128] = jnp.broadcast_to(total, (256, 128))
        acc[half, :, LAT + 128 :] = jnp.broadcast_to(top, (256, 128))

    new_part(1 - core)
    swap = pltpu.make_async_remote_copy(
        acc.at[1 - core], sib, ss_c, rs_c, device_id=sibling, device_id_type=MESH
    )
    swap.start()
    new_part(core)
    swap.wait_recv()

    def far_copy(i, to):
        return pltpu.make_async_remote_copy(
            piece.at[to, pl.ds(0, 33)], got.at[i, pl.ds(0, 33)], ss_a.at[i], rs_a.at[i],
            device_id=(s, to * 2 + core), device_id_type=MESH,
        )

    lanes = lax.broadcasted_iota(jnp.int32, (64, 128), 1)
    spot = lax.rem(lax.broadcasted_iota(jnp.int32, (64, 128), 0), 8)
    for k in range(4):
        chips = (1 - z if k < 2 else z) * 16 + (k % 2) * 8
        rows = pl.ds(pl.multiple_of(chips * 8, 64), 64)
        total_a, total_b = acc[core, rows, LAT : LAT + 128], sib[rows, LAT : LAT + 128]
        top_a, top_b = acc[core, rows, LAT + 128 :], sib[rows, LAT + 128 :]
        top = jnp.maximum(top_a, top_b)
        fa, fb = jnp.exp(top_a - top), jnp.exp(top_b - top)
        for t in range(4):
            cols = slice(t * 128, (t + 1) * 128)
            merged = acc[core, rows, cols] * fa + sib[rows, cols] * fb
            piece[pl.ds(chips, 8), t * 8 : (t + 1) * 8, :] = merged.reshape(8, 8, 128)
        meta = jnp.where(lanes == spot, total_a * fa + total_b * fb, jnp.where(lanes == spot + 8, top, 0.0))
        piece[pl.ds(chips, 8), 32:33, :] = jnp.sum(meta.reshape(8, 8, 128), axis=1, keepdims=True)

        def far_start(p, carry):
            to = chips + p
            i = (
                lax.rem(to // 16 - z + 2, 2) * 16
                + lax.rem(lax.rem(to // 4, 4) - xx + 4, 4) * 4
                + lax.rem(lax.rem(to, 4) - y + 4, 4)
            )

            @pl.when(to != chip)
            def _():
                far_copy(i, to).start()

            return carry

        lax.fori_loop(0, 8, far_start, 0)

    got[0] = piece[chip]
    swap.wait_send()
    for copy in right_copies + left_copies:
        copy.wait_send()

    def far_wait(i, carry):
        far_copy(i, far_chip(i)).wait()
        return carry

    lax.fori_loop(1, 32, far_wait, 0)

    meta = got[:, 32]
    share = pltpu.roll(jnp.exp(meta - jnp.max(meta, axis=0, keepdims=True)), 120, 1)
    diagonal = lane8 == lax.broadcasted_iota(jnp.int32, (8, 128), 0)

    def column(line):
        return jnp.sum(jnp.where(diagonal, line, 0.0), axis=1, keepdims=True)

    total = column(jnp.sum(meta * share, axis=0, keepdims=True))
    number = [jnp.zeros((8, 128), f32)] * 4
    for i in range(32):
        factor = column(share[i : i + 1])
        number = [v + got[i, t * 8 : (t + 1) * 8] * factor for t, v in enumerate(number)]
    inverse = 1.0 / total
    out[...] = jnp.concatenate([v * inverse for v in number], axis=1).astype(bf16)


def body(prompt, kv_down, latent_gain, block_home, block_slot, latent_cache, cache_lengths, queries, new_rows):
    f32, bf16 = jnp.float32, jnp.bfloat16
    any_space = pl.BlockSpec(memory_space=pl.ANY)
    n_loads = 15
    dma = pltpu.SemaphoreType.DMA
    msg = (PIECE, 8, 128)
    out = pl.pallas_call(
        kernel,
        out_shape=jax.ShapeDtypeStruct((8, LAT), bf16),
        in_specs=[any_space] * 11,
        out_specs=pl.BlockSpec(memory_space=pltpu.VMEM),
        scratch_shapes=[
            pltpu.VMEM((2, 4, BLK // 2, prompt.shape[1]), bf16),
            pltpu.VMEM((640, kv_down.shape[0]), bf16),
            pltpu.VMEM((4 * NCH,) + msg, f32),
            pltpu.VMEM((MSGS,) + msg, f32),
            pltpu.VMEM((MSGS,) + msg, f32),
            pltpu.VMEM((MSGS,) + msg, f32),
            pltpu.VMEM((MSGS,) + msg, f32),
            pltpu.VMEM((1, LAT), f32),
            pltpu.VMEM((384, 128), f32),
            pltpu.SMEM((4,), jnp.int32),
            pltpu.SMEM((4,), jnp.int32),
            pltpu.SMEM((2,), jnp.int32),
            pltpu.VMEM((256, TABLE), jnp.int32),
            pltpu.VMEM((1, TABLE), jnp.int32),
            pltpu.SMEM((1, TABLE), jnp.int32),
            pltpu.VMEM((2, WIDE, CSLOT), bf16),
            pltpu.VMEM((2, 2, 640, 128), bf16),
            pltpu.VMEM((2, 256, 640), bf16),
            pltpu.VMEM((2, 2, WIDE), bf16),
            pltpu.VMEM((128, WIDE), f32),
            pltpu.VMEM((2 * BLK, 640), bf16),
            pltpu.VMEM((2, 256, 768), f32),
            pltpu.VMEM((256, 768), f32),
            pltpu.VMEM((32, 40, 128), f32),
            pltpu.VMEM((32, 40, 128), f32),
            dma((n_loads,)),
            dma((MSGS * len(SPLITS),)),
            dma((MSGS * len(SPLITS),)),
            dma((MSGS * len(SPLITS),)),
            dma((MSGS * len(SPLITS),)),
            dma,
            dma,
            dma((32,)),
            dma((32,)),
        ],
        compiler_params=pltpu.CompilerParams(
            collective_id=0, has_side_effects=True, vmem_limit_bytes=62 * 1024 * 1024
        ),
        name="mla_decode",
    )(
        prompt.reshape(4, 2, BLK // 2, prompt.shape[1]), kv_down.T, latent_gain.reshape(1, LAT), block_home, block_slot, latent_cache.transpose(0, 2, 1),
        cache_lengths, queries.transpose(0, 2, 3, 1), new_rows,
        jnp.asarray(plan_table()), jnp.asarray(turn_tables()),
    )
    return out.reshape(2, 2, 2, LAT)


def solution(mesh):
    placed = (
        P("seq", "section"),
        P("section", None),
        P(),
        P("seq"),
        P("seq"),
        P("section", "seq", None),
        P("section"),
        P("section", None, None, None),
        P("section", None, None),
    )
    return jax.shard_map(body, mesh=mesh, in_specs=placed, out_specs=P("section", "seq", None, None), check_vma=False)
```

```python
import functools

import jax
import jax.numpy as jnp
import numpy as np
from jax import lax
from jax.experimental import pallas as pl
from jax.experimental.pallas import tpu as pltpu
from jax.sharding import PartitionSpec as P

MESH = pl.DeviceIdType.MESH
LAT = 512
WIDE = 576
BLK = 128
CSLOT = 256
SCALE = 192.0 ** (-0.5)
EPS = 1e-6
BIG = 1e30

ROWS = 16
NCH = BLK // ROWS
LAG = 8
SHORT = 4
EXTRA = 2
MSGS = 2 * NCH + EXTRA
SLOT = 40
PIECE = 9
SPLITS = ((0, PIECE),)
TABLE = 128


def chunk_id(block, chunk):
    half = NCH // 2
    return (chunk // half) * (4 * half) + block * half + chunk % half


def passes(rel):
    n_right, n_left = rel.count(1), rel.count(3)
    opposite = [b for b in range(4) if rel[b] == 2]
    if len(opposite) == 1:
        right = 1 if n_right <= n_left else 0
    else:
        right = 1 + (n_left == 2) - (n_right == 2)
    right = min(max(right, 0), len(opposite))
    items = [(b, j) for j in range(NCH) for b in opposite]
    if len(opposite) == 2 and right == 2:
        return items[EXTRA:], items[:EXTRA]
    if len(opposite) == 2 and right == 0:
        return items[:EXTRA], items[EXTRA:]
    return [v for v in items if v[0] in opposite[:right]], [v for v in items if v[0] in opposite[right:]]


def lane_plan(rel, side):
    near, step = (1, 1) if side == 0 else (3, -1)
    mine = passes(rel)[side]
    behind = passes([(r + step) % 4 for r in rel])[side]
    spots = {i: v + (0,) for i, v in enumerate(mine)}
    many = len(behind) > LAG
    for i, v in enumerate(behind):
        at = i + (SHORT if many else LAG)
        spots[at] = v + (2 if many else 1,)
    plain = [(b, j) for j in range(NCH) for b in range(4) if rel[b] == near and (b, j) not in behind]
    free = [m for m in range(MSGS) if m not in spots]
    spots.update({m: v + (0,) for m, v in zip(free, plain)})
    return spots


@functools.lru_cache(None)
def plan_table():
    table = np.zeros((256, TABLE), np.int32)
    for code in range(256):
        rel = [(code >> (2 * b)) & 3 for b in range(4)]
        if max(rel.count(g) for g in range(4)) > 2:
            continue
        for side in range(2):
            for m, (b, j, adds) in lane_plan(rel, side).items():
                table[code, m] |= (chunk_id(b, j) | (adds << 5)) << (7 * side)
        owned = [b for b in range(4) if rel[b] == 0]
        from_left = lane_plan([(r + 1) % 4 for r in rel], 0)
        from_right = lane_plan([(r - 1) % 4 for r in rel], 1)
        for k, b in enumerate(owned):
            for j in range(NCH):
                at_left = [m for m, v in from_left.items() if v[:2] == (b, j)][0]
                at_right = [m for m, v in from_right.items() if v[:2] == (b, j)][0]
                table[code, MSGS + k * NCH + j] = chunk_id(b, j) | (at_left << 5) | (at_right << 10)
    return table


@functools.lru_cache(None)
def turn_tables():
    lane = np.arange(128)
    inverse = 10000.0 ** (-2.0 * (lane % 32) / 64.0)
    base = (np.arange(128) * 128.0)[:, None] * inverse[None, :]
    row = np.arange(8 * NCH)
    inside = ((row // 8) * 16 + row % 8)[:, None] + np.where(lane < 64, 0, 8)[None, :]
    inside = inside * inverse[None, :]
    both = np.concatenate([np.cos(base), np.sin(base), np.cos(inside), np.sin(inside)], axis=0)
    return both.astype(np.float32)


def kernel(
    prompt, kv_down, gain, home, slot, cache, lengths, queries, news, plan, turns,
    out,
    x, w, part, send_r, send_l, recv_r, recv_l,
    gain_v, turn_v, home_s, slot_s, len_s, plan_v, row_v, plan_s,
    keys, qt, q, news_v, news_f, fresh, acc, sib, scale, metas, piece, got,
    in_sem, ss_r, ss_l, rs_r, rs_l, ss_c, rs_c, ss_a, rs_a, here,
):
    f32, bf16 = jnp.float32, jnp.bfloat16
    s = lax.axis_index("section")
    c = lax.axis_index("seq")
    core = lax.rem(c, 2)
    chip = c // 2
    y, xx, z = lax.rem(chip, 4), lax.rem(chip // 4, 4), chip // 16
    right, left = (lax.rem(s + 1, 4), c), (lax.rem(s + 3, 4), c)
    sibling = (s, chip * 2 + (1 - core))

    def at_chip(dx, dy, dz):
        to = lax.rem(z + dz, 2) * 16 + lax.rem(xx + dx, 4) * 4 + lax.rem(y + dy, 4)
        return (s, to * 2 + core)

    def tell(sem, devices):
        for device in devices:
            pl.semaphore_signal(sem, inc=1, device_id=device, device_id_type=MESH)

    x_near, y_near, z_near = [at_chip(1, 0, 0), at_chip(3, 0, 0)], [at_chip(0, 1, 0), at_chip(0, 3, 0)], [at_chip(0, 0, 1)]
    barrier = pltpu.get_barrier_semaphore()
    tell(barrier, [right, left] + x_near + y_near + z_near + [sibling])

    loads = []

    def load(src, dst):
        copy = pltpu.make_async_copy(src, dst, in_sem.at[len(loads)])
        copy.start()
        loads.append(copy)
        return copy

    first = [
        load(kv_down, w.at[pl.ds(0, WIDE)]),
        load(prompt.at[:, 0], x.at[0]),
        load(kv_down.at[pl.ds(LAT, 64)], w.at[pl.ds(WIDE, 64)]),
    ]
    small = [load(home, home_s), load(plan, plan_v)]
    second = [load(prompt.at[:, 1], x.at[1])]

    lane8 = lax.broadcasted_iota(jnp.int32, (8, 128), 1)
    lane_low = lane8 < 64

    def dot_t(a, b):
        return lax.dot_general(a, b, (((1,), (1,)), ((), ())), preferred_element_type=f32)

    def project(half):
        both = dot_t(x[half].reshape(256, x.shape[3]), w[...])
        main, turn = both[:, :LAT], both[:, LAT:]
        n = 4 * (BLK // 2) // ROWS
        main = main.reshape(n, 2, 8, LAT)
        turn = turn.reshape(n, 2, 8, 128)
        for h in range(2):
            for t in range(4):
                part[half * n : (half + 1) * n, h * 5 + t] = main[:, h, :, t * 128 : (t + 1) * 128]
        part[half * n : (half + 1) * n, 4] = jnp.where(lane_low[None], turn[:, 0], turn[:, 1])

    for copy in small:
        copy.wait()
    code = jnp.int32(0)
    for b in range(4):
        group = home_s[b] // 2
        code = code + lax.rem(group - s + 4, 4) * (4**b)
    row_v[...] = plan_v[pl.ds(code, 1)]
    row_copy = load(row_v, plan_s)

    third = [
        load(slot, slot_s),
        load(lengths, len_s),
        load(cache, keys),
        load(news, news_v),
        load(gain, gain_v),
        load(turns, turn_v),
        load(queries, qt.at[:, :, pl.ds(0, WIDE)]),
        load(queries.at[:, :, pl.ds(LAT, 64)], qt.at[:, :, pl.ds(WIDE, 64)]),
    ]
    for copy in first:
        copy.wait()
    project(0)
    row_copy.wait()
    pl.semaphore_wait(barrier, 8)
    tell(here.at[0], x_near)

    right_copies, left_copies = [], []

    def message(m):
        word = plan_s[0, m]
        for part_at, tiles in SPLITS:
            for side, (buf, got_buf, copies, ss, rs, device) in enumerate(
                (
                    (send_r, recv_r, right_copies, ss_r, rs_r, right),
                    (send_l, recv_l, left_copies, ss_l, rs_l, left),
                )
            ):
                field = word >> (7 * side)
                value = part[field & 31, pl.ds(part_at, tiles)]
                at = len(copies)
                adds = (field >> 5) & 3
                if m >= SHORT:
                    copies[m - SHORT].wait_recv()
                    value = value + jnp.where(adds == 2, got_buf[m - SHORT], 0.0)
                if m >= LAG:
                    value = value + jnp.where(adds == 1, got_buf[m - LAG], 0.0)
                buf[m, pl.ds(part_at, tiles)] = value
                copy = pltpu.make_async_remote_copy(
                    buf.at[m, pl.ds(part_at, tiles)],
                    got_buf.at[m, pl.ds(part_at, tiles)],
                    ss.at[at],
                    rs.at[at],
                    device_id=device,
                    device_id_type=MESH,
                )
                copy.start()
                copies.append(copy)

    for m in range(NCH // 2):
        message(m)
    for copy in second:
        copy.wait()
    project(1)
    for m in range(NCH // 2, LAG):
        message(m)
    pl.semaphore_wait(here.at[0], 2)
    tell(here.at[1], y_near)
    for copy in third:
        copy.wait()

    owned = jnp.int32(0)
    slot_block = [jnp.int32(0), jnp.int32(0)]
    slot_turn = [jnp.int32(0), jnp.int32(0)]
    slot_req = [jnp.int32(-1), jnp.int32(-1)]
    written = [jnp.int32(0)] * 4
    for b in range(4):
        is_mine = home_s[b] // 2 == s
        req = lax.rem(home_s[b], 2)
        target = req * 2 + slot_s[b]
        for k in range(2):
            take = is_mine & (owned == k)
            slot_req[k] = jnp.where(take, req, slot_req[k])
            slot_turn[k] = jnp.where(take, slot_s[b], slot_turn[k])
        for t in range(4):
            written[t] = jnp.where(is_mine & (target == t), 1, written[t])
        owned = owned + jnp.where(is_mine, 1, 0)

    row = lax.broadcasted_iota(jnp.int32, (256, 1), 0)
    row_req = lax.rem(row, 8) // 4
    row_new = lax.rem(row, 2)
    row_chip = row // 8

    n_keys = 2 * CSLOT + 128
    col = lax.broadcasted_iota(jnp.int32, (1, n_keys), 1)
    cblk = col // 128
    is_written = jnp.where(cblk == 0, written[0], jnp.where(cblk == 1, written[1], jnp.where(cblk == 2, written[2], written[3])))
    length = jnp.where(col < CSLOT, len_s[0], len_s[1])
    pos = c * CSLOT + lax.rem(col, CSLOT)
    col_req = jnp.where((col < 2 * CSLOT) & (pos < length) & (is_written == 0), col // CSLOT, -1)
    own_col = col - 2 * CSLOT
    own_code = jnp.where((own_col >= 0) & (own_col < 4), own_col, -9)

    def order_queries(half):
        i = lax.broadcasted_iota(jnp.int32, (256, 1), 0)
        head = (i // 8) * 4 + half * 2 + lax.rem(i // 2, 2)
        pick = lax.broadcasted_iota(jnp.int32, (256, 128), 1)
        rows = jnp.zeros((256, 640), f32)
        for r in range(2):
            for n in range(2):
                wanted = jnp.where((lax.rem(i // 4, 2) == r) & (lax.rem(i, 2) == n), head, -1)
                rows = rows + dot_t(jnp.where(pick == wanted, 1.0, 0.0).astype(bf16), qt[r, n])
        q[half] = rows.astype(bf16)

    def old_part(half):
        rows = q[half, :, :WIDE]
        scores = jnp.concatenate(
            [
                jnp.dot(rows, keys[0], preferred_element_type=f32),
                jnp.dot(rows, keys[1], preferred_element_type=f32),
                dot_t(rows, news_f[...].astype(bf16)),
            ],
            axis=1,
        )
        scores = scores * SCALE
        here = jnp.where((half == core) & (row_chip == chip), 1, 0)
        mask = (col_req == row_req) | (
            (own_code // 2 == row_req) & (lax.rem(own_code, 2) <= row_new) & (own_code >= 0) & (here == 1)
        )
        top = jnp.max(jnp.where(mask, scores, -BIG), axis=1, keepdims=True)
        weight = jnp.where(mask, jnp.exp(scores - top), 0.0).astype(bf16)
        total = jnp.sum(weight.astype(f32), axis=1, keepdims=True)
        acc[half, :, :LAT] = (
            dot_t(weight[:, :CSLOT], keys[0, :LAT])
            + dot_t(weight[:, CSLOT : 2 * CSLOT], keys[1, :LAT])
            + jnp.dot(weight[:, 2 * CSLOT :], news_f[:, :LAT].astype(bf16), preferred_element_type=f32)
        )
        acc[half, :, LAT : LAT + 128] = jnp.broadcast_to(total, (256, 128))
        acc[half, :, LAT + 128 :] = jnp.broadcast_to(top, (256, 128))

    news_f[...] = jnp.zeros_like(news_f)
    for r in range(2):
        news_f[2 * r : 2 * r + 2] = news_v[r].astype(f32)
    order_queries(1 - core)
    order_queries(core)
    message(LAG)
    message(LAG + 1)
    old_part(1 - core)
    message(LAG + 2)
    old_part(core)
    pl.semaphore_wait(here.at[1], 2)
    tell(here.at[2], y_near)
    for m in range(LAG + 3, LAG + 6):
        message(m)
    pl.semaphore_wait(here.at[2], 2)
    tell(here.at[3], z_near)
    for m in range(LAG + 6, MSGS):
        message(m)
    pl.semaphore_wait(here.at[3], 1)
    for at in range(MSGS - SHORT, MSGS):
        right_copies[at].wait_recv()
        left_copies[at].wait_recv()

    sign = jnp.where(lax.rem(lane8, 64) < 32, -1.0, 1.0)
    near_half = lax.rem(lane8, 64) < 32
    gain_row = gain_v[...]
    for k in range(2):
        turn_at = c * 2 + slot_turn[k]
        cos_b = turn_v[pl.ds(turn_at, 1)]
        sin_b = turn_v[pl.ds(turn_at + 128, 1)]
        for j in range(NCH):
            word = plan_s[0, MSGS + k * NCH + j]
            value = part[word & 31] + recv_r[(word >> 5) & 31] + recv_l[(word >> 10) & 31]
            for h in range(2):
                pieces = [value[h * 5 + t] for t in range(4)]
                square = pieces[0] * pieces[0]
                for t in range(1, 4):
                    square = square + pieces[t] * pieces[t]
                factor = lax.rsqrt(jnp.sum(square, axis=1, keepdims=True) * (1.0 / LAT) + EPS)
                pieces = [p * factor * gain_row[:, t * 128 : (t + 1) * 128] for t, p in enumerate(pieces)]
                if h == 0:
                    upper = pieces
            cos_i = turn_v[256 + j * 8 : 256 + (j + 1) * 8]
            sin_i = turn_v[320 + j * 8 : 320 + (j + 1) * 8]
            cosine = cos_b * cos_i - sin_b * sin_i
            sine = (sin_b * cos_i + cos_b * sin_i) * sign
            rotary = value[4]
            swapped = jnp.where(near_half, pltpu.roll(rotary, 96, 1), pltpu.roll(rotary, 32, 1))
            turned = rotary * cosine + swapped * sine
            at = k * BLK + j * ROWS
            for t in range(4):
                fresh[at : at + ROWS, t * 128 : (t + 1) * 128] = jnp.concatenate([upper[t], pieces[t]], axis=0).astype(bf16)
            fresh[at : at + ROWS, LAT:] = jnp.concatenate(
                [jnp.where(lane_low, turned, 0.0), jnp.where(lane_low, 0.0, turned)], axis=0
            ).astype(bf16)

    fcol = lax.broadcasted_iota(jnp.int32, (1, 2 * BLK), 1)
    fresh_req = jnp.where(fcol < BLK, slot_req[0], slot_req[1])

    def new_part(half):
        scores = lax.dot_general(q[half], fresh[...], (((1,), (1,)), ((), ())), preferred_element_type=f32)
        scores = scores * SCALE
        mask = fresh_req == row_req
        old_total = acc[half, :, LAT : LAT + 1]
        old_top = acc[half, :, LAT + 128 : LAT + 129]
        top = jnp.maximum(jnp.max(jnp.where(mask, scores, -BIG), axis=1, keepdims=True), old_top)
        weight = jnp.where(mask, jnp.exp(scores - top), 0.0).astype(bf16)
        shrink = jnp.exp(old_top - top)
        total = jnp.sum(weight.astype(f32), axis=1, keepdims=True) + old_total * shrink
        acc[half, :, :LAT] = acc[half, :, :LAT] * shrink + jnp.dot(
            weight, fresh[:, :LAT], preferred_element_type=f32
        )
        acc[half, :, LAT : LAT + 128] = jnp.broadcast_to(total, (256, 128))
        acc[half, :, LAT + 128 :] = jnp.broadcast_to(top, (256, 128))

    new_part(1 - core)
    swap = pltpu.make_async_remote_copy(
        acc.at[1 - core], sib, ss_c, rs_c, device_id=sibling, device_id_type=MESH
    )
    swap.start()
    new_part(core)
    swap.wait_recv()

    lanes = lax.broadcasted_iota(jnp.int32, (256, 128), 1)
    spot = lax.rem(lax.broadcasted_iota(jnp.int32, (256, 128), 0), 8)
    total_a, total_b = acc[core, :, LAT : LAT + 128], sib[:, LAT : LAT + 128]
    top_a, top_b = acc[core, :, LAT + 128 :], sib[:, LAT + 128 :]
    top = jnp.maximum(top_a, top_b)
    fa, fb = jnp.exp(top_a - top), jnp.exp(top_b - top)
    scale[0], scale[1] = fa, fb
    meta = jnp.where(lanes == spot, total_a * fa + total_b * fb, jnp.where(lanes == spot + 8, top, 0.0))
    metas[...] = jnp.sum(meta.reshape(32, 8, 128), axis=1)

    def hops(i):
        dx, dy = (i // 4) % 4, i % 4
        return i // 16 + min(dx, 4 - dx) + min(dy, 4 - dy)

    for i in sorted(range(32), key=hops, reverse=True):
        _, to = at_chip((i // 4) % 4, i % 4, i // 16)
        to = to // 2
        rows = pl.ds(pl.multiple_of(to * 8, 8), 8)
        store = piece if i else got
        fa, fb = scale[0, rows], scale[1, rows]
        for t in range(4):
            cols = slice(t * 128, (t + 1) * 128)
            store[i * SLOT + t * 8 : i * SLOT + (t + 1) * 8] = acc[core, rows, cols] * fa + sib[rows, cols] * fb
        store[i * SLOT + 32 : i * SLOT + 33] = metas[pl.ds(to, 1)]
        if i:
            pltpu.make_async_remote_copy(
                piece.at[pl.ds(i * SLOT, 33)], got.at[pl.ds(i * SLOT, 33)], ss_a, rs_a,
                device_id=(s, to * 2 + core), device_id_type=MESH,
            ).start()

    swap.wait_send()
    for copy in right_copies + left_copies:
        copy.wait_send()
    every = pltpu.make_async_remote_copy(
        piece.at[pl.ds(0, 31 * 33)], got.at[pl.ds(0, 31 * 33)], ss_a, rs_a, device_id=sibling, device_id_type=MESH
    )
    every.wait_recv()
    every.wait_send()

    meta = got[pl.ds(32, 32, stride=SLOT)]
    share = pltpu.roll(jnp.exp(meta - jnp.max(meta, axis=0, keepdims=True)), 120, 1)
    diagonal = lane8 == lax.broadcasted_iota(jnp.int32, (8, 128), 0)

    def column(line):
        return jnp.sum(jnp.where(diagonal, line, 0.0), axis=1, keepdims=True)

    total = column(jnp.sum(meta * share, axis=0, keepdims=True))
    number = [jnp.zeros((8, 128), f32)] * 4
    for i in range(32):
        factor = column(share[i : i + 1])
        number = [v + got[i * SLOT + t * 8 : i * SLOT + (t + 1) * 8] * factor for t, v in enumerate(number)]
    inverse = 1.0 / total
    out[...] = jnp.concatenate([v * inverse for v in number], axis=1).astype(bf16)


def body(prompt, kv_down, latent_gain, block_home, block_slot, latent_cache, cache_lengths, queries, new_rows):
    f32, bf16 = jnp.float32, jnp.bfloat16
    any_space = pl.BlockSpec(memory_space=pl.ANY)
    n_loads = 15
    dma = pltpu.SemaphoreType.DMA
    msg = (PIECE, 8, 128)
    out = pl.pallas_call(
        kernel,
        out_shape=jax.ShapeDtypeStruct((8, LAT), bf16),
        in_specs=[any_space] * 11,
        out_specs=pl.BlockSpec(memory_space=pltpu.VMEM),
        scratch_shapes=[
            pltpu.VMEM((2, 4, BLK // 2, prompt.shape[1]), bf16),
            pltpu.VMEM((640, kv_down.shape[0]), bf16),
            pltpu.VMEM((4 * NCH,) + msg, f32),
            pltpu.VMEM((MSGS,) + msg, f32),
            pltpu.VMEM((MSGS,) + msg, f32),
            pltpu.VMEM((MSGS,) + msg, f32),
            pltpu.VMEM((MSGS,) + msg, f32),
            pltpu.VMEM((1, LAT), f32),
            pltpu.VMEM((384, 128), f32),
            pltpu.SMEM((4,), jnp.int32),
            pltpu.SMEM((4,), jnp.int32),
            pltpu.SMEM((2,), jnp.int32),
            pltpu.VMEM((256, TABLE), jnp.int32),
            pltpu.VMEM((1, TABLE), jnp.int32),
            pltpu.SMEM((1, TABLE), jnp.int32),
            pltpu.VMEM((2, WIDE, CSLOT), bf16),
            pltpu.VMEM((2, 2, 640, 128), bf16),
            pltpu.VMEM((2, 256, 640), bf16),
            pltpu.VMEM((2, 2, WIDE), bf16),
            pltpu.VMEM((128, WIDE), f32),
            pltpu.VMEM((2 * BLK, 640), bf16),
            pltpu.VMEM((2, 256, 768), f32),
            pltpu.VMEM((256, 768), f32),
            pltpu.VMEM((2, 256, 128), f32),
            pltpu.VMEM((32, 128), f32),
            pltpu.VMEM((32 * SLOT, 128), f32),
            pltpu.VMEM((32 * SLOT, 128), f32),
            dma((n_loads,)),
            dma((MSGS * len(SPLITS),)),
            dma((MSGS * len(SPLITS),)),
            dma((MSGS * len(SPLITS),)),
            dma((MSGS * len(SPLITS),)),
            dma,
            dma,
            dma,
            dma,
            pltpu.SemaphoreType.REGULAR((4,)),
        ],
        compiler_params=pltpu.CompilerParams(
            collective_id=0, has_side_effects=True, vmem_limit_bytes=62 * 1024 * 1024
        ),
        name="mla_decode",
    )(
        prompt.reshape(4, 2, BLK // 2, prompt.shape[1]), kv_down.T, latent_gain.reshape(1, LAT), block_home, block_slot, latent_cache.transpose(0, 2, 1),
        cache_lengths, queries.transpose(0, 2, 3, 1), new_rows,
        jnp.asarray(plan_table()), jnp.asarray(turn_tables()),
    )
    return out.reshape(2, 2, 2, LAT)


def solution(mesh):
    placed = (
        P("seq", "section"),
        P("section", None),
        P(),
        P("seq"),
        P("seq"),
        P("section", "seq", None),
        P("section"),
        P("section", None, None, None),
        P("section", None, None),
    )
    return jax.shard_map(body, mesh=mesh, in_specs=placed, out_specs=P("section", "seq", None, None), check_vma=False)
```

```python
import functools

import jax
import jax.numpy as jnp
import numpy as np
from jax import lax
from jax.experimental import pallas as pl
from jax.experimental.pallas import tpu as pltpu
from jax.sharding import PartitionSpec as P

MESH = pl.DeviceIdType.MESH
LAT = 512
WIDE = 576
BLK = 128
CSLOT = 256
SCALE = 192.0 ** (-0.5)
EPS = 1e-6
BIG = 1e30

ROWS = 16
NCH = BLK // ROWS
LAG = 8
SHORT = 4
EXTRA = 2
MSGS = 2 * NCH + EXTRA
SLOT = 40
PIECE = 9
SPLITS = ((0, PIECE),)
TABLE = 128


def chunk_id(block, chunk):
    half = NCH // 2
    return (chunk // half) * (4 * half) + block * half + chunk % half


def passes(rel):
    n_right, n_left = rel.count(1), rel.count(3)
    opposite = [b for b in range(4) if rel[b] == 2]
    if len(opposite) == 1:
        right = 1 if n_right <= n_left else 0
    else:
        right = 1 + (n_left == 2) - (n_right == 2)
    right = min(max(right, 0), len(opposite))
    items = [(b, j) for j in range(NCH) for b in opposite]
    if len(opposite) == 2 and right == 2:
        return items[EXTRA:], items[:EXTRA]
    if len(opposite) == 2 and right == 0:
        return items[:EXTRA], items[EXTRA:]
    return [v for v in items if v[0] in opposite[:right]], [v for v in items if v[0] in opposite[right:]]


def lane_plan(rel, side):
    near, step = (1, 1) if side == 0 else (3, -1)
    mine = passes(rel)[side]
    behind = passes([(r + step) % 4 for r in rel])[side]
    spots = {i: v + (0,) for i, v in enumerate(mine)}
    many = len(behind) > LAG
    for i, v in enumerate(behind):
        at = i + (SHORT if many else LAG)
        spots[at] = v + (2 if many else 1,)
    plain = [(b, j) for j in range(NCH) for b in range(4) if rel[b] == near and (b, j) not in behind]
    free = [m for m in range(MSGS) if m not in spots]
    spots.update({m: v + (0,) for m, v in zip(free, plain)})
    return spots


@functools.lru_cache(None)
def plan_table():
    table = np.zeros((256, TABLE), np.int32)
    for code in range(256):
        rel = [(code >> (2 * b)) & 3 for b in range(4)]
        if max(rel.count(g) for g in range(4)) > 2:
            continue
        for side in range(2):
            for m, (b, j, adds) in lane_plan(rel, side).items():
                table[code, m] |= (chunk_id(b, j) | (adds << 5)) << (7 * side)
        owned = [b for b in range(4) if rel[b] == 0]
        from_left = lane_plan([(r + 1) % 4 for r in rel], 0)
        from_right = lane_plan([(r - 1) % 4 for r in rel], 1)
        for k, b in enumerate(owned):
            for j in range(NCH):
                at_left = [m for m, v in from_left.items() if v[:2] == (b, j)][0]
                at_right = [m for m, v in from_right.items() if v[:2] == (b, j)][0]
                table[code, MSGS + k * NCH + j] = chunk_id(b, j) | (at_left << 5) | (at_right << 10)
    return table


@functools.lru_cache(None)
def turn_tables():
    lane = np.arange(128)
    inverse = 10000.0 ** (-2.0 * (lane % 32) / 64.0)
    base = (np.arange(128) * 128.0)[:, None] * inverse[None, :]
    row = np.arange(8 * NCH)
    inside = ((row // 8) * 16 + row % 8)[:, None] + np.where(lane < 64, 0, 8)[None, :]
    inside = inside * inverse[None, :]
    both = np.concatenate([np.cos(base), np.sin(base), np.cos(inside), np.sin(inside)], axis=0)
    return both.astype(np.float32)


def kernel(
    prompt, kv_down, gain, home, slot, cache, lengths, queries, news, plan, turns,
    out,
    x, w, part, send_r, send_l, recv_r, recv_l,
    gain_v, turn_v, home_s, slot_s, len_s, plan_v, row_v, plan_s,
    keys, qt, q, news_v, news_f, fresh, acc, sib, scale, metas, piece, got,
    in_sem, ss_r, ss_l, rs_r, rs_l, ss_c, rs_c, ss_a, rs_a, here,
):
    f32, bf16 = jnp.float32, jnp.bfloat16
    s = lax.axis_index("section")
    c = lax.axis_index("seq")
    core = lax.rem(c, 2)
    chip = c // 2
    y, xx, z = lax.rem(chip, 4), lax.rem(chip // 4, 4), chip // 16
    right, left = (lax.rem(s + 1, 4), c), (lax.rem(s + 3, 4), c)
    sibling = (s, chip * 2 + (1 - core))

    def at_chip(dx, dy, dz):
        to = lax.rem(z + dz, 2) * 16 + lax.rem(xx + dx, 4) * 4 + lax.rem(y + dy, 4)
        return (s, to * 2 + core)

    def tell(sem, devices):
        for device in devices:
            pl.semaphore_signal(sem, inc=1, device_id=device, device_id_type=MESH)

    x_near, y_near, z_near = [at_chip(1, 0, 0), at_chip(3, 0, 0)], [at_chip(0, 1, 0), at_chip(0, 3, 0)], [at_chip(0, 0, 1)]
    barrier = pltpu.get_barrier_semaphore()
    tell(barrier, [right, left] + x_near + y_near + z_near + [sibling])

    loads = []

    def load(src, dst):
        copy = pltpu.make_async_copy(src, dst, in_sem.at[len(loads)])
        copy.start()
        loads.append(copy)
        return copy

    first = [
        load(kv_down, w.at[pl.ds(0, WIDE)]),
        load(prompt.at[:, 0], x.at[0]),
        load(kv_down.at[pl.ds(LAT, 64)], w.at[pl.ds(WIDE, 64)]),
    ]
    small = [load(home, home_s), load(plan, plan_v)]
    second = [load(prompt.at[:, 1], x.at[1])]

    lane8 = lax.broadcasted_iota(jnp.int32, (8, 128), 1)
    lane_low = lane8 < 64

    def dot_t(a, b):
        return lax.dot_general(a, b, (((1,), (1,)), ((), ())), preferred_element_type=f32)

    def project(half):
        both = dot_t(x[half].reshape(256, x.shape[3]), w[...])
        main, turn = both[:, :LAT], both[:, LAT:]
        n = 4 * (BLK // 2) // ROWS
        main = main.reshape(n, 2, 8, LAT)
        turn = turn.reshape(n, 2, 8, 128)
        for h in range(2):
            for t in range(4):
                part[half * n : (half + 1) * n, h * 5 + t] = main[:, h, :, t * 128 : (t + 1) * 128]
        part[half * n : (half + 1) * n, 4] = jnp.where(lane_low[None], turn[:, 0], turn[:, 1])

    for copy in small:
        copy.wait()
    code = jnp.int32(0)
    for b in range(4):
        group = home_s[b] // 2
        code = code + lax.rem(group - s + 4, 4) * (4**b)
    row_v[...] = plan_v[pl.ds(code, 1)]
    row_copy = load(row_v, plan_s)

    third = [
        load(slot, slot_s),
        load(lengths, len_s),
        load(cache, keys),
        load(news, news_v),
        load(gain, gain_v),
        load(turns, turn_v),
        load(queries, qt.at[:, :, pl.ds(0, WIDE)]),
        load(queries.at[:, :, pl.ds(LAT, 64)], qt.at[:, :, pl.ds(WIDE, 64)]),
    ]
    for copy in first:
        copy.wait()
    project(0)
    row_copy.wait()
    pl.semaphore_wait(barrier, 8)
    tell(here.at[0], x_near)

    right_copies, left_copies = [], []

    def message(m):
        word = plan_s[0, m]
        for part_at, tiles in SPLITS:
            for side, (buf, got_buf, copies, ss, rs, device) in enumerate(
                (
                    (send_r, recv_r, right_copies, ss_r, rs_r, right),
                    (send_l, recv_l, left_copies, ss_l, rs_l, left),
                )
            ):
                field = word >> (7 * side)
                value = part[field & 31, pl.ds(part_at, tiles)]
                at = len(copies)
                adds = (field >> 5) & 3
                if m >= SHORT:
                    copies[m - SHORT].wait_recv()
                    value = value + jnp.where(adds == 2, got_buf[m - SHORT], 0.0)
                if m >= LAG:
                    value = value + jnp.where(adds == 1, got_buf[m - LAG], 0.0)
                buf[m, pl.ds(part_at, tiles)] = value
                copy = pltpu.make_async_remote_copy(
                    buf.at[m, pl.ds(part_at, tiles)],
                    got_buf.at[m, pl.ds(part_at, tiles)],
                    ss.at[at],
                    rs.at[at],
                    device_id=device,
                    device_id_type=MESH,
                )
                copy.start()
                copies.append(copy)

    for m in range(NCH // 2):
        message(m)
    for copy in second:
        copy.wait()
    project(1)
    for m in range(NCH // 2, LAG):
        message(m)
    pl.semaphore_wait(here.at[0], 2)
    tell(here.at[1], y_near)
    for copy in third:
        copy.wait()

    owned = jnp.int32(0)
    slot_block = [jnp.int32(0), jnp.int32(0)]
    slot_turn = [jnp.int32(0), jnp.int32(0)]
    slot_req = [jnp.int32(-1), jnp.int32(-1)]
    written = [jnp.int32(0)] * 4
    for b in range(4):
        is_mine = home_s[b] // 2 == s
        req = lax.rem(home_s[b], 2)
        target = req * 2 + slot_s[b]
        for k in range(2):
            take = is_mine & (owned == k)
            slot_req[k] = jnp.where(take, req, slot_req[k])
            slot_turn[k] = jnp.where(take, slot_s[b], slot_turn[k])
        for t in range(4):
            written[t] = jnp.where(is_mine & (target == t), 1, written[t])
        owned = owned + jnp.where(is_mine, 1, 0)

    row = lax.broadcasted_iota(jnp.int32, (256, 1), 0)
    row_req = lax.rem(row, 8) // 4
    row_new = lax.rem(row, 2)
    row_chip = row // 8

    n_keys = 2 * CSLOT + 128
    col = lax.broadcasted_iota(jnp.int32, (1, n_keys), 1)
    cblk = col // 128
    is_written = jnp.where(cblk == 0, written[0], jnp.where(cblk == 1, written[1], jnp.where(cblk == 2, written[2], written[3])))
    length = jnp.where(col < CSLOT, len_s[0], len_s[1])
    pos = c * CSLOT + lax.rem(col, CSLOT)
    col_req = jnp.where((col < 2 * CSLOT) & (pos < length) & (is_written == 0), col // CSLOT, -1)
    own_col = col - 2 * CSLOT
    own_code = jnp.where((own_col >= 0) & (own_col < 4), own_col, -9)

    def order_queries(half):
        i = lax.broadcasted_iota(jnp.int32, (256, 1), 0)
        head = (i // 8) * 4 + half * 2 + lax.rem(i // 2, 2)
        pick = lax.broadcasted_iota(jnp.int32, (256, 128), 1)
        rows = jnp.zeros((256, 640), f32)
        for r in range(2):
            for n in range(2):
                wanted = jnp.where((lax.rem(i // 4, 2) == r) & (lax.rem(i, 2) == n), head, -1)
                rows = rows + dot_t(jnp.where(pick == wanted, 1.0, 0.0).astype(bf16), qt[r, n])
        q[half] = rows.astype(bf16)

    def old_part(half):
        rows = q[half, :, :WIDE]
        scores = jnp.concatenate(
            [
                jnp.dot(rows, keys[0], preferred_element_type=f32),
                jnp.dot(rows, keys[1], preferred_element_type=f32),
                dot_t(rows, news_f[...].astype(bf16)),
            ],
            axis=1,
        )
        scores = scores * SCALE
        here = jnp.where((half == core) & (row_chip == chip), 1, 0)
        mask = (col_req == row_req) | (
            (own_code // 2 == row_req) & (lax.rem(own_code, 2) <= row_new) & (own_code >= 0) & (here == 1)
        )
        top = jnp.max(jnp.where(mask, scores, -BIG), axis=1, keepdims=True)
        weight = jnp.where(mask, jnp.exp(scores - top), 0.0).astype(bf16)
        total = jnp.sum(weight.astype(f32), axis=1, keepdims=True)
        acc[half, :, :LAT] = (
            dot_t(weight[:, :CSLOT], keys[0, :LAT])
            + dot_t(weight[:, CSLOT : 2 * CSLOT], keys[1, :LAT])
            + jnp.dot(weight[:, 2 * CSLOT :], news_f[:, :LAT].astype(bf16), preferred_element_type=f32)
        )
        lanes = lax.broadcasted_iota(jnp.int32, (256, 128), 1)
        acc[half, :, LAT:] = jnp.where(lanes < 64, total, top)

    news_f[...] = jnp.zeros_like(news_f)
    for r in range(2):
        news_f[2 * r : 2 * r + 2] = news_v[r].astype(f32)
    order_queries(1 - core)
    order_queries(core)
    message(LAG)
    message(LAG + 1)
    old_part(1 - core)
    message(LAG + 2)
    old_part(core)
    pl.semaphore_wait(here.at[1], 2)
    tell(here.at[2], y_near)
    for m in range(LAG + 3, LAG + 6):
        message(m)
    pl.semaphore_wait(here.at[2], 2)
    tell(here.at[3], z_near)
    for m in range(LAG + 6, MSGS):
        message(m)
    pl.semaphore_wait(here.at[3], 1)
    for at in range(MSGS - SHORT, MSGS):
        right_copies[at].wait_recv()
        left_copies[at].wait_recv()

    sign = jnp.where(lax.rem(lane8, 64) < 32, -1.0, 1.0)
    near_half = lax.rem(lane8, 64) < 32
    gain_row = gain_v[...]
    for k in range(2):
        turn_at = c * 2 + slot_turn[k]
        cos_b = turn_v[pl.ds(turn_at, 1)]
        sin_b = turn_v[pl.ds(turn_at + 128, 1)]
        for j in range(NCH):
            word = plan_s[0, MSGS + k * NCH + j]
            value = part[word & 31] + recv_r[(word >> 5) & 31] + recv_l[(word >> 10) & 31]
            for h in range(2):
                pieces = [value[h * 5 + t] for t in range(4)]
                square = pieces[0] * pieces[0]
                for t in range(1, 4):
                    square = square + pieces[t] * pieces[t]
                factor = lax.rsqrt(jnp.sum(square, axis=1, keepdims=True) * (1.0 / LAT) + EPS)
                pieces = [p * factor * gain_row[:, t * 128 : (t + 1) * 128] for t, p in enumerate(pieces)]
                if h == 0:
                    upper = pieces
            cos_i = turn_v[256 + j * 8 : 256 + (j + 1) * 8]
            sin_i = turn_v[320 + j * 8 : 320 + (j + 1) * 8]
            cosine = cos_b * cos_i - sin_b * sin_i
            sine = (sin_b * cos_i + cos_b * sin_i) * sign
            rotary = value[4]
            swapped = jnp.where(near_half, pltpu.roll(rotary, 96, 1), pltpu.roll(rotary, 32, 1))
            turned = rotary * cosine + swapped * sine
            at = k * BLK + j * ROWS
            for t in range(4):
                fresh[at : at + ROWS, t * 128 : (t + 1) * 128] = jnp.concatenate([upper[t], pieces[t]], axis=0).astype(bf16)
            fresh[at : at + ROWS, LAT:] = jnp.concatenate(
                [jnp.where(lane_low, turned, 0.0), jnp.where(lane_low, 0.0, turned)], axis=0
            ).astype(bf16)

    fcol = lax.broadcasted_iota(jnp.int32, (1, 2 * BLK), 1)
    fresh_req = jnp.where(fcol < BLK, slot_req[0], slot_req[1])

    low = lax.broadcasted_iota(jnp.int32, (128, 128), 1) < 64

    def rows_of(plane):
        return pl.ds(pl.multiple_of(plane * 128, 128), 128)

    def new_part(half, plane):
        rows = rows_of(plane)
        scores = dot_t(q[half, rows], fresh[...]) * SCALE
        mask = fresh_req == row_req[:128]
        old_total = acc[half, rows, LAT : LAT + 1]
        old_top = acc[half, rows, LAT + 64 : LAT + 65]
        top = jnp.maximum(jnp.max(jnp.where(mask, scores, -BIG), axis=1, keepdims=True), old_top)
        weight = jnp.where(mask, jnp.exp(scores - top), 0.0).astype(bf16)
        shrink = jnp.exp(old_top - top)
        total = jnp.sum(weight.astype(f32), axis=1, keepdims=True) + old_total * shrink
        acc[half, rows, :LAT] = acc[half, rows, :LAT] * shrink + jnp.dot(
            weight, fresh[:, :LAT], preferred_element_type=f32
        )
        acc[half, rows, LAT:] = jnp.where(low, total, top)

    planes = (1 - z, z)
    swaps = []
    for k, plane in enumerate(planes):
        new_part(1 - core, plane)
        swap = pltpu.make_async_remote_copy(
            acc.at[1 - core, rows_of(plane)], sib.at[rows_of(plane)], ss_c.at[k], rs_c.at[k],
            device_id=sibling, device_id_type=MESH,
        )
        swap.start()
        swaps.append(swap)
    for plane in planes:
        new_part(core, plane)

    lanes = lax.broadcasted_iota(jnp.int32, (128, 128), 1)
    spot = lax.rem(lax.broadcasted_iota(jnp.int32, (128, 128), 0), 8)

    def merge_scales(plane):
        rows = rows_of(plane)
        meta_a, meta_b = acc[core, rows, LAT:], sib[rows, LAT:]
        total_a, total_b = meta_a[:, :1], meta_b[:, :1]
        top_a, top_b = meta_a[:, 64:65], meta_b[:, 64:65]
        top = jnp.maximum(top_a, top_b)
        fa, fb = jnp.exp(top_a - top), jnp.exp(top_b - top)
        scale[0, rows] = jnp.broadcast_to(fa, (128, 128))
        scale[1, rows] = jnp.broadcast_to(fb, (128, 128))
        meta = jnp.where(lanes == spot, total_a * fa + total_b * fb, jnp.where(lanes == spot + 8, top, 0.0))
        metas[pl.ds(pl.multiple_of(plane * 16, 16), 16)] = jnp.sum(meta.reshape(16, 8, 128), axis=1)

    def hops(i):
        dx, dy = (i // 4) % 4, i % 4
        return i // 16 + min(dx, 4 - dx) + min(dy, 4 - dy)

    order = sorted(range(16, 32), key=hops, reverse=True) + sorted(range(16), key=hops, reverse=True)
    for at, i in enumerate(order):
        if at % 16 == 0:
            swaps[at // 16].wait_recv()
            merge_scales(planes[at // 16])
        _, to = at_chip((i // 4) % 4, i % 4, i // 16)
        to = to // 2
        rows = pl.ds(pl.multiple_of(to * 8, 8), 8)
        store = piece if i else got
        fa, fb = scale[0, rows], scale[1, rows]
        for t in range(4):
            cols = slice(t * 128, (t + 1) * 128)
            store[i * SLOT + t * 8 : i * SLOT + (t + 1) * 8] = acc[core, rows, cols] * fa + sib[rows, cols] * fb
        store[i * SLOT + 32 : i * SLOT + 33] = metas[pl.ds(to, 1)]
        if i:
            pltpu.make_async_remote_copy(
                piece.at[pl.ds(i * SLOT, 33)], got.at[pl.ds(i * SLOT, 33)], ss_a, rs_a,
                device_id=(s, to * 2 + core), device_id_type=MESH,
            ).start()

    for swap in swaps:
        swap.wait_send()
    for copy in right_copies + left_copies:
        copy.wait_send()
    every = pltpu.make_async_remote_copy(
        piece.at[pl.ds(0, 31 * 33)], got.at[pl.ds(0, 31 * 33)], ss_a, rs_a, device_id=sibling, device_id_type=MESH
    )
    every.wait_recv()
    every.wait_send()

    meta = got[pl.ds(32, 32, stride=SLOT)]
    share = pltpu.roll(jnp.exp(meta - jnp.max(meta, axis=0, keepdims=True)), 120, 1)
    diagonal = lane8 == lax.broadcasted_iota(jnp.int32, (8, 128), 0)

    def column(line):
        return jnp.sum(jnp.where(diagonal, line, 0.0), axis=1, keepdims=True)

    total = column(jnp.sum(meta * share, axis=0, keepdims=True))
    number = [jnp.zeros((8, 128), f32)] * 4
    for i in range(32):
        factor = column(share[i : i + 1])
        number = [v + got[i * SLOT + t * 8 : i * SLOT + (t + 1) * 8] * factor for t, v in enumerate(number)]
    inverse = 1.0 / total
    out[...] = jnp.concatenate([v * inverse for v in number], axis=1).astype(bf16)


def body(prompt, kv_down, latent_gain, block_home, block_slot, latent_cache, cache_lengths, queries, new_rows):
    f32, bf16 = jnp.float32, jnp.bfloat16
    any_space = pl.BlockSpec(memory_space=pl.ANY)
    n_loads = 15
    dma = pltpu.SemaphoreType.DMA
    msg = (PIECE, 8, 128)
    out = pl.pallas_call(
        kernel,
        out_shape=jax.ShapeDtypeStruct((8, LAT), bf16),
        in_specs=[any_space] * 11,
        out_specs=pl.BlockSpec(memory_space=pltpu.VMEM),
        scratch_shapes=[
            pltpu.VMEM((2, 4, BLK // 2, prompt.shape[1]), bf16),
            pltpu.VMEM((640, kv_down.shape[0]), bf16),
            pltpu.VMEM((4 * NCH,) + msg, f32),
            pltpu.VMEM((MSGS,) + msg, f32),
            pltpu.VMEM((MSGS,) + msg, f32),
            pltpu.VMEM((MSGS,) + msg, f32),
            pltpu.VMEM((MSGS,) + msg, f32),
            pltpu.VMEM((1, LAT), f32),
            pltpu.VMEM((384, 128), f32),
            pltpu.SMEM((4,), jnp.int32),
            pltpu.SMEM((4,), jnp.int32),
            pltpu.SMEM((2,), jnp.int32),
            pltpu.VMEM((256, TABLE), jnp.int32),
            pltpu.VMEM((1, TABLE), jnp.int32),
            pltpu.SMEM((1, TABLE), jnp.int32),
            pltpu.VMEM((2, WIDE, CSLOT), bf16),
            pltpu.VMEM((2, 2, 640, 128), bf16),
            pltpu.VMEM((2, 256, 640), bf16),
            pltpu.VMEM((2, 2, WIDE), bf16),
            pltpu.VMEM((128, WIDE), f32),
            pltpu.VMEM((2 * BLK, 640), bf16),
            pltpu.VMEM((2, 256, 640), f32),
            pltpu.VMEM((256, 640), f32),
            pltpu.VMEM((2, 256, 128), f32),
            pltpu.VMEM((32, 128), f32),
            pltpu.VMEM((32 * SLOT, 128), f32),
            pltpu.VMEM((32 * SLOT, 128), f32),
            dma((n_loads,)),
            dma((MSGS * len(SPLITS),)),
            dma((MSGS * len(SPLITS),)),
            dma((MSGS * len(SPLITS),)),
            dma((MSGS * len(SPLITS),)),
            dma((2,)),
            dma((2,)),
            dma,
            dma,
            pltpu.SemaphoreType.REGULAR((4,)),
        ],
        compiler_params=pltpu.CompilerParams(
            collective_id=0, has_side_effects=True, vmem_limit_bytes=62 * 1024 * 1024
        ),
        name="mla_decode",
    )(
        prompt.reshape(4, 2, BLK // 2, prompt.shape[1]), kv_down.T, latent_gain.reshape(1, LAT), block_home, block_slot, latent_cache.transpose(0, 2, 1),
        cache_lengths, queries.transpose(0, 2, 3, 1), new_rows,
        jnp.asarray(plan_table()), jnp.asarray(turn_tables()),
    )
    return out.reshape(2, 2, 2, LAT)


def solution(mesh):
    placed = (
        P("seq", "section"),
        P("section", None),
        P(),
        P("seq"),
        P("seq"),
        P("section", "seq", None),
        P("section"),
        P("section", None, None, None),
        P("section", None, None),
    )
    return jax.shard_map(body, mesh=mesh, in_specs=placed, out_specs=P("section", "seq", None, None), check_vma=False)
```

```python
import functools

import jax
import jax.numpy as jnp
import numpy as np
from jax import lax
from jax.experimental import pallas as pl
from jax.experimental.pallas import tpu as pltpu
from jax.sharding import PartitionSpec as P

MESH = pl.DeviceIdType.MESH
LAT = 512
WIDE = 576
BLK = 128
CSLOT = 256
SCALE = 192.0 ** (-0.5)
EPS = 1e-6
BIG = 1e30

ROWS = 16
NCH = BLK // ROWS
LAG = 8
SHORT = 4
EXTRA = 2
MSGS = 2 * NCH + EXTRA
SLOT = 40
PIECE = 9
SPLITS = ((0, PIECE),)
TABLE = 128


def chunk_id(block, chunk):
    half = NCH // 2
    return (chunk // half) * (4 * half) + block * half + chunk % half


def passes(rel):
    n_right, n_left = rel.count(1), rel.count(3)
    opposite = [b for b in range(4) if rel[b] == 2]
    if len(opposite) == 1:
        right = 1 if n_right <= n_left else 0
    else:
        right = 1 + (n_left == 2) - (n_right == 2)
    right = min(max(right, 0), len(opposite))
    items = [(b, j) for j in range(NCH) for b in opposite]
    if len(opposite) == 2 and right == 2:
        return items[EXTRA:], items[:EXTRA]
    if len(opposite) == 2 and right == 0:
        return items[:EXTRA], items[EXTRA:]
    return [v for v in items if v[0] in opposite[:right]], [v for v in items if v[0] in opposite[right:]]


def lane_plan(rel, side):
    near, step = (1, 1) if side == 0 else (3, -1)
    mine = passes(rel)[side]
    behind = passes([(r + step) % 4 for r in rel])[side]
    spots = {i: v + (0,) for i, v in enumerate(mine)}
    many = len(behind) > LAG
    for i, v in enumerate(behind):
        at = i + (SHORT if many else LAG)
        spots[at] = v + (2 if many else 1,)
    plain = [(b, j) for j in range(NCH) for b in range(4) if rel[b] == near and (b, j) not in behind]
    free = [m for m in range(MSGS) if m not in spots]
    spots.update({m: v + (0,) for m, v in zip(free, plain)})
    return spots


@functools.lru_cache(None)
def plan_table():
    table = np.zeros((256, TABLE), np.int32)
    for code in range(256):
        rel = [(code >> (2 * b)) & 3 for b in range(4)]
        if max(rel.count(g) for g in range(4)) > 2:
            continue
        for side in range(2):
            for m, (b, j, adds) in lane_plan(rel, side).items():
                table[code, m] |= (chunk_id(b, j) | (adds << 5)) << (7 * side)
        owned = [b for b in range(4) if rel[b] == 0]
        from_left = lane_plan([(r + 1) % 4 for r in rel], 0)
        from_right = lane_plan([(r - 1) % 4 for r in rel], 1)
        for k, b in enumerate(owned):
            for j in range(NCH):
                at_left = [m for m, v in from_left.items() if v[:2] == (b, j)][0]
                at_right = [m for m, v in from_right.items() if v[:2] == (b, j)][0]
                table[code, MSGS + k * NCH + j] = chunk_id(b, j) | (at_left << 5) | (at_right << 10)
    return table


@functools.lru_cache(None)
def turn_tables():
    lane = np.arange(128)
    inverse = 10000.0 ** (-2.0 * (lane % 32) / 64.0)
    base = (np.arange(128) * 128.0)[:, None] * inverse[None, :]
    row = np.arange(8 * NCH)
    inside = ((row // 8) * 16 + row % 8)[:, None] + np.where(lane < 64, 0, 8)[None, :]
    inside = inside * inverse[None, :]
    both = np.concatenate([np.cos(base), np.sin(base), np.cos(inside), np.sin(inside)], axis=0)
    return both.astype(np.float32)


def kernel(
    prompt, kv_down, gain, home, slot, cache, lengths, queries, news, plan, turns,
    out,
    x, w, part, send_r, send_l, recv_r, recv_l,
    gain_v, turn_v, home_s, slot_s, len_s, plan_v, row_v, plan_s,
    keys, qt, q, news_v, news_f, fresh, acc, sib, scale, metas, piece, got,
    in_sem, ss_r, ss_l, rs_r, rs_l, ss_c, rs_c, ss_a, rs_a, here,
):
    f32, bf16 = jnp.float32, jnp.bfloat16
    s = lax.axis_index("section")
    c = lax.axis_index("seq")
    core = lax.rem(c, 2)
    chip = c // 2
    y, xx, z = lax.rem(chip, 4), lax.rem(chip // 4, 4), chip // 16
    right, left = (lax.rem(s + 1, 4), c), (lax.rem(s + 3, 4), c)
    sibling = (s, chip * 2 + (1 - core))

    def at_chip(dx, dy, dz):
        to = lax.rem(z + dz, 2) * 16 + lax.rem(xx + dx, 4) * 4 + lax.rem(y + dy, 4)
        return (s, to * 2 + core)

    def tell(sem, devices):
        for device in devices:
            pl.semaphore_signal(sem, inc=1, device_id=device, device_id_type=MESH)

    x_near, y_near, z_near = [at_chip(1, 0, 0), at_chip(3, 0, 0)], [at_chip(0, 1, 0), at_chip(0, 3, 0)], [at_chip(0, 0, 1)]
    barrier = pltpu.get_barrier_semaphore()
    tell(barrier, [right, left] + x_near + y_near + z_near + [sibling])

    loads = []

    def load(src, dst):
        copy = pltpu.make_async_copy(src, dst, in_sem.at[len(loads)])
        copy.start()
        loads.append(copy)
        return copy

    first = [
        load(kv_down, w.at[pl.ds(0, WIDE)]),
        load(prompt.at[:, 0], x.at[0]),
        load(kv_down.at[pl.ds(LAT, 64)], w.at[pl.ds(WIDE, 64)]),
    ]
    small = [load(home, home_s), load(plan, plan_v)]
    second = [load(prompt.at[:, 1], x.at[1])]

    lane8 = lax.broadcasted_iota(jnp.int32, (8, 128), 1)
    lane_low = lane8 < 64

    def dot_t(a, b):
        return lax.dot_general(a, b, (((1,), (1,)), ((), ())), preferred_element_type=f32)

    def project(half):
        both = dot_t(x[half].reshape(256, x.shape[3]), w[...])
        main, turn = both[:, :LAT], both[:, LAT:]
        n = 4 * (BLK // 2) // ROWS
        main = main.reshape(n, 2, 8, LAT)
        turn = turn.reshape(n, 2, 8, 128)
        for h in range(2):
            for t in range(4):
                part[half * n : (half + 1) * n, h * 5 + t] = main[:, h, :, t * 128 : (t + 1) * 128]
        part[half * n : (half + 1) * n, 4] = jnp.where(lane_low[None], turn[:, 0], turn[:, 1])

    for copy in small:
        copy.wait()
    code = jnp.int32(0)
    for b in range(4):
        group = home_s[b] // 2
        code = code + lax.rem(group - s + 4, 4) * (4**b)
    row_v[...] = plan_v[pl.ds(code, 1)]
    row_copy = load(row_v, plan_s)

    third = [
        load(slot, slot_s),
        load(lengths, len_s),
        load(cache, keys),
        load(news, news_v),
        load(gain, gain_v),
        load(turns, turn_v),
        load(queries, qt.at[:, :, pl.ds(0, WIDE)]),
        load(queries.at[:, :, pl.ds(LAT, 64)], qt.at[:, :, pl.ds(WIDE, 64)]),
    ]
    for copy in first:
        copy.wait()
    project(0)
    row_copy.wait()
    pl.semaphore_wait(barrier, 8)
    tell(here.at[0], x_near)

    right_copies, left_copies = [], []

    def message(m):
        word = plan_s[0, m]
        for part_at, tiles in SPLITS:
            for side, (buf, got_buf, copies, ss, rs, device) in enumerate(
                (
                    (send_r, recv_r, right_copies, ss_r, rs_r, right),
                    (send_l, recv_l, left_copies, ss_l, rs_l, left),
                )
            ):
                field = word >> (7 * side)
                value = part[field & 31, pl.ds(part_at, tiles)]
                at = len(copies)
                adds = (field >> 5) & 3
                if m >= SHORT:
                    copies[m - SHORT].wait_recv()
                    value = value + jnp.where(adds == 2, got_buf[m - SHORT], 0.0)
                if m >= LAG:
                    value = value + jnp.where(adds == 1, got_buf[m - LAG], 0.0)
                buf[m, pl.ds(part_at, tiles)] = value
                copy = pltpu.make_async_remote_copy(
                    buf.at[m, pl.ds(part_at, tiles)],
                    got_buf.at[m, pl.ds(part_at, tiles)],
                    ss.at[at],
                    rs.at[at],
                    device_id=device,
                    device_id_type=MESH,
                )
                copy.start()
                copies.append(copy)

    for m in range(NCH // 2):
        message(m)
    for copy in second:
        copy.wait()
    project(1)
    for m in range(NCH // 2, LAG):
        message(m)
    pl.semaphore_wait(here.at[0], 2)
    tell(here.at[1], y_near)
    for copy in third:
        copy.wait()

    owned = jnp.int32(0)
    slot_block = [jnp.int32(0), jnp.int32(0)]
    slot_turn = [jnp.int32(0), jnp.int32(0)]
    slot_req = [jnp.int32(-1), jnp.int32(-1)]
    written = [jnp.int32(0)] * 4
    for b in range(4):
        is_mine = home_s[b] // 2 == s
        req = lax.rem(home_s[b], 2)
        target = req * 2 + slot_s[b]
        for k in range(2):
            take = is_mine & (owned == k)
            slot_req[k] = jnp.where(take, req, slot_req[k])
            slot_turn[k] = jnp.where(take, slot_s[b], slot_turn[k])
        for t in range(4):
            written[t] = jnp.where(is_mine & (target == t), 1, written[t])
        owned = owned + jnp.where(is_mine, 1, 0)

    row = lax.broadcasted_iota(jnp.int32, (256, 1), 0)
    row_req = lax.rem(row, 8) // 4
    row_new = lax.rem(row, 2)
    row_chip = row // 8

    n_keys = 2 * CSLOT + 128
    col = lax.broadcasted_iota(jnp.int32, (1, n_keys), 1)
    cblk = col // 128
    is_written = jnp.where(cblk == 0, written[0], jnp.where(cblk == 1, written[1], jnp.where(cblk == 2, written[2], written[3])))
    length = jnp.where(col < CSLOT, len_s[0], len_s[1])
    pos = c * CSLOT + lax.rem(col, CSLOT)
    col_req = jnp.where((col < 2 * CSLOT) & (pos < length) & (is_written == 0), col // CSLOT, -1)
    own_col = col - 2 * CSLOT
    own_code = jnp.where((own_col >= 0) & (own_col < 4), own_col, -9)

    def order_queries(half):
        i = lax.broadcasted_iota(jnp.int32, (256, 1), 0)
        head = (i // 8) * 4 + half * 2 + lax.rem(i // 2, 2)
        pick = lax.broadcasted_iota(jnp.int32, (256, 128), 1)
        rows = jnp.zeros((256, 640), f32)
        for r in range(2):
            for n in range(2):
                wanted = jnp.where((lax.rem(i // 4, 2) == r) & (lax.rem(i, 2) == n), head, -1)
                rows = rows + dot_t(jnp.where(pick == wanted, 1.0, 0.0).astype(bf16), qt[r, n])
        q[half] = rows.astype(bf16)

    def old_part(half):
        rows = q[half, :, :WIDE]
        scores = jnp.concatenate(
            [
                jnp.dot(rows, keys[0], preferred_element_type=f32),
                jnp.dot(rows, keys[1], preferred_element_type=f32),
                dot_t(rows, news_f[...].astype(bf16)),
            ],
            axis=1,
        )
        scores = scores * SCALE
        here = jnp.where((half == core) & (row_chip == chip), 1, 0)
        mask = (col_req == row_req) | (
            (own_code // 2 == row_req) & (lax.rem(own_code, 2) <= row_new) & (own_code >= 0) & (here == 1)
        )
        top = jnp.max(jnp.where(mask, scores, -BIG), axis=1, keepdims=True)
        weight = jnp.where(mask, jnp.exp(scores - top), 0.0).astype(bf16)
        total = jnp.sum(weight.astype(f32), axis=1, keepdims=True)
        acc[half, :, :LAT] = (
            dot_t(weight[:, :CSLOT], keys[0, :LAT])
            + dot_t(weight[:, CSLOT : 2 * CSLOT], keys[1, :LAT])
            + jnp.dot(weight[:, 2 * CSLOT :], news_f[:, :LAT].astype(bf16), preferred_element_type=f32)
        )
        lanes = lax.broadcasted_iota(jnp.int32, (256, 128), 1)
        acc[half, :, LAT:] = jnp.where(lanes < 64, total, top)

    news_f[...] = jnp.zeros_like(news_f)
    for r in range(2):
        news_f[2 * r : 2 * r + 2] = news_v[r].astype(f32)
    message(LAG)
    order_queries(1 - core)
    message(LAG + 1)
    order_queries(core)
    message(LAG + 2)
    old_part(1 - core)
    pl.semaphore_wait(here.at[1], 2)
    tell(here.at[2], y_near)
    message(LAG + 3)
    old_part(core)
    for m in range(LAG + 4, LAG + 6):
        message(m)
    pl.semaphore_wait(here.at[2], 2)
    tell(here.at[3], z_near)
    for m in range(LAG + 6, MSGS):
        message(m)
    pl.semaphore_wait(here.at[3], 1)
    for at in range(MSGS - SHORT, MSGS):
        right_copies[at].wait_recv()
        left_copies[at].wait_recv()

    sign = jnp.where(lax.rem(lane8, 64) < 32, -1.0, 1.0)
    near_half = lax.rem(lane8, 64) < 32
    gain_row = gain_v[...]
    for k in range(2):
        turn_at = c * 2 + slot_turn[k]
        cos_b = turn_v[pl.ds(turn_at, 1)]
        sin_b = turn_v[pl.ds(turn_at + 128, 1)]
        for j in range(NCH):
            word = plan_s[0, MSGS + k * NCH + j]
            value = part[word & 31] + recv_r[(word >> 5) & 31] + recv_l[(word >> 10) & 31]
            for h in range(2):
                pieces = [value[h * 5 + t] for t in range(4)]
                square = pieces[0] * pieces[0]
                for t in range(1, 4):
                    square = square + pieces[t] * pieces[t]
                factor = lax.rsqrt(jnp.sum(square, axis=1, keepdims=True) * (1.0 / LAT) + EPS)
                pieces = [p * factor * gain_row[:, t * 128 : (t + 1) * 128] for t, p in enumerate(pieces)]
                if h == 0:
                    upper = pieces
            cos_i = turn_v[256 + j * 8 : 256 + (j + 1) * 8]
            sin_i = turn_v[320 + j * 8 : 320 + (j + 1) * 8]
            cosine = cos_b * cos_i - sin_b * sin_i
            sine = (sin_b * cos_i + cos_b * sin_i) * sign
            rotary = value[4]
            swapped = jnp.where(near_half, pltpu.roll(rotary, 96, 1), pltpu.roll(rotary, 32, 1))
            turned = rotary * cosine + swapped * sine
            at = k * BLK + j * ROWS
            for t in range(4):
                fresh[at : at + ROWS, t * 128 : (t + 1) * 128] = jnp.concatenate([upper[t], pieces[t]], axis=0).astype(bf16)
            fresh[at : at + ROWS, LAT:] = jnp.concatenate(
                [jnp.where(lane_low, turned, 0.0), jnp.where(lane_low, 0.0, turned)], axis=0
            ).astype(bf16)

    fcol = lax.broadcasted_iota(jnp.int32, (1, 2 * BLK), 1)
    fresh_req = jnp.where(fcol < BLK, slot_req[0], slot_req[1])

    low = lax.broadcasted_iota(jnp.int32, (128, 128), 1) < 64

    def rows_of(plane):
        return pl.ds(pl.multiple_of(plane * 128, 128), 128)

    def new_part(half, plane):
        rows = rows_of(plane)
        scores = dot_t(q[half, rows], fresh[...]) * SCALE
        mask = fresh_req == row_req[:128]
        old_total = acc[half, rows, LAT : LAT + 1]
        old_top = acc[half, rows, LAT + 64 : LAT + 65]
        top = jnp.maximum(jnp.max(jnp.where(mask, scores, -BIG), axis=1, keepdims=True), old_top)
        weight = jnp.where(mask, jnp.exp(scores - top), 0.0).astype(bf16)
        shrink = jnp.exp(old_top - top)
        total = jnp.sum(weight.astype(f32), axis=1, keepdims=True) + old_total * shrink
        acc[half, rows, :LAT] = acc[half, rows, :LAT] * shrink + jnp.dot(
            weight, fresh[:, :LAT], preferred_element_type=f32
        )
        acc[half, rows, LAT:] = jnp.where(low, total, top)

    planes = (1 - z, z)
    swaps = []
    for k, plane in enumerate(planes):
        new_part(1 - core, plane)
        swap = pltpu.make_async_remote_copy(
            acc.at[1 - core, rows_of(plane)], sib.at[rows_of(plane)], ss_c.at[k], rs_c.at[k],
            device_id=sibling, device_id_type=MESH,
        )
        swap.start()
        swaps.append(swap)

    lanes = lax.broadcasted_iota(jnp.int32, (128, 128), 1)
    spot = lax.rem(lax.broadcasted_iota(jnp.int32, (128, 128), 0), 8)

    def merge_scales(plane):
        rows = rows_of(plane)
        meta_a, meta_b = acc[core, rows, LAT:], sib[rows, LAT:]
        total_a, total_b = meta_a[:, :1], meta_b[:, :1]
        top_a, top_b = meta_a[:, 64:65], meta_b[:, 64:65]
        top = jnp.maximum(top_a, top_b)
        fa, fb = jnp.exp(top_a - top), jnp.exp(top_b - top)
        scale[0, rows] = jnp.broadcast_to(fa, (128, 128))
        scale[1, rows] = jnp.broadcast_to(fb, (128, 128))
        meta = jnp.where(lanes == spot, total_a * fa + total_b * fb, jnp.where(lanes == spot + 8, top, 0.0))
        metas[pl.ds(pl.multiple_of(plane * 16, 16), 16)] = jnp.sum(meta.reshape(16, 8, 128), axis=1)

    def hops(i):
        dx, dy = (i // 4) % 4, i % 4
        return i // 16 + min(dx, 4 - dx) + min(dy, 4 - dy)

    order = sorted(range(16, 32), key=hops, reverse=True) + sorted(range(16), key=hops, reverse=True)
    for at, i in enumerate(order):
        if at % 16 == 0:
            new_part(core, planes[at // 16])
            swaps[at // 16].wait_recv()
            merge_scales(planes[at // 16])
        _, to = at_chip((i // 4) % 4, i % 4, i // 16)
        to = to // 2
        rows = pl.ds(pl.multiple_of(to * 8, 8), 8)
        store = piece if i else got
        fa, fb = scale[0, rows], scale[1, rows]
        for t in range(4):
            cols = slice(t * 128, (t + 1) * 128)
            store[i * SLOT + t * 8 : i * SLOT + (t + 1) * 8] = acc[core, rows, cols] * fa + sib[rows, cols] * fb
        store[i * SLOT + 32 : i * SLOT + 33] = metas[pl.ds(to, 1)]
        if i:
            pltpu.make_async_remote_copy(
                piece.at[pl.ds(i * SLOT, 33)], got.at[pl.ds(i * SLOT, 33)], ss_a, rs_a,
                device_id=(s, to * 2 + core), device_id_type=MESH,
            ).start()

    for swap in swaps:
        swap.wait_send()
    for copy in right_copies + left_copies:
        copy.wait_send()
    every = pltpu.make_async_remote_copy(
        piece.at[pl.ds(0, 31 * 33)], got.at[pl.ds(0, 31 * 33)], ss_a, rs_a, device_id=sibling, device_id_type=MESH
    )
    every.wait_recv()
    every.wait_send()

    meta = got[pl.ds(32, 32, stride=SLOT)]
    share = pltpu.roll(jnp.exp(meta - jnp.max(meta, axis=0, keepdims=True)), 120, 1)
    diagonal = lane8 == lax.broadcasted_iota(jnp.int32, (8, 128), 0)

    def column(line):
        return jnp.sum(jnp.where(diagonal, line, 0.0), axis=1, keepdims=True)

    total = column(jnp.sum(meta * share, axis=0, keepdims=True))
    number = [jnp.zeros((8, 128), f32)] * 4
    for i in range(32):
        factor = column(share[i : i + 1])
        number = [v + got[i * SLOT + t * 8 : i * SLOT + (t + 1) * 8] * factor for t, v in enumerate(number)]
    inverse = 1.0 / total
    out[...] = jnp.concatenate([v * inverse for v in number], axis=1).astype(bf16)


def body(prompt, kv_down, latent_gain, block_home, block_slot, latent_cache, cache_lengths, queries, new_rows):
    f32, bf16 = jnp.float32, jnp.bfloat16
    any_space = pl.BlockSpec(memory_space=pl.ANY)
    n_loads = 15
    dma = pltpu.SemaphoreType.DMA
    msg = (PIECE, 8, 128)
    out = pl.pallas_call(
        kernel,
        out_shape=jax.ShapeDtypeStruct((8, LAT), bf16),
        in_specs=[any_space] * 11,
        out_specs=pl.BlockSpec(memory_space=pltpu.VMEM),
        scratch_shapes=[
            pltpu.VMEM((2, 4, BLK // 2, prompt.shape[1]), bf16),
            pltpu.VMEM((640, kv_down.shape[0]), bf16),
            pltpu.VMEM((4 * NCH,) + msg, f32),
            pltpu.VMEM((MSGS,) + msg, f32),
            pltpu.VMEM((MSGS,) + msg, f32),
            pltpu.VMEM((MSGS,) + msg, f32),
            pltpu.VMEM((MSGS,) + msg, f32),
            pltpu.VMEM((1, LAT), f32),
            pltpu.VMEM((384, 128), f32),
            pltpu.SMEM((4,), jnp.int32),
            pltpu.SMEM((4,), jnp.int32),
            pltpu.SMEM((2,), jnp.int32),
            pltpu.VMEM((256, TABLE), jnp.int32),
            pltpu.VMEM((1, TABLE), jnp.int32),
            pltpu.SMEM((1, TABLE), jnp.int32),
            pltpu.VMEM((2, WIDE, CSLOT), bf16),
            pltpu.VMEM((2, 2, 640, 128), bf16),
            pltpu.VMEM((2, 256, 640), bf16),
            pltpu.VMEM((2, 2, WIDE), bf16),
            pltpu.VMEM((128, WIDE), f32),
            pltpu.VMEM((2 * BLK, 640), bf16),
            pltpu.VMEM((2, 256, 640), f32),
            pltpu.VMEM((256, 640), f32),
            pltpu.VMEM((2, 256, 128), f32),
            pltpu.VMEM((32, 128), f32),
            pltpu.VMEM((32 * SLOT, 128), f32),
            pltpu.VMEM((32 * SLOT, 128), f32),
            dma((n_loads,)),
            dma((MSGS * len(SPLITS),)),
            dma((MSGS * len(SPLITS),)),
            dma((MSGS * len(SPLITS),)),
            dma((MSGS * len(SPLITS),)),
            dma((2,)),
            dma((2,)),
            dma,
            dma,
            pltpu.SemaphoreType.REGULAR((4,)),
        ],
        compiler_params=pltpu.CompilerParams(
            collective_id=0, has_side_effects=True, vmem_limit_bytes=62 * 1024 * 1024
        ),
        name="mla_decode",
    )(
        prompt.reshape(4, 2, BLK // 2, prompt.shape[1]), kv_down.T, latent_gain.reshape(1, LAT), block_home, block_slot, latent_cache.transpose(0, 2, 1),
        cache_lengths, queries.transpose(0, 2, 3, 1), new_rows,
        jnp.asarray(plan_table()), jnp.asarray(turn_tables()),
    )
    return out.reshape(2, 2, 2, LAT)


def solution(mesh):
    placed = (
        P("seq", "section"),
        P("section", None),
        P(),
        P("seq"),
        P("seq"),
        P("section", "seq", None),
        P("section"),
        P("section", None, None, None),
        P("section", None, None),
    )
    return jax.shard_map(body, mesh=mesh, in_specs=placed, out_specs=P("section", "seq", None, None), check_vma=False)
```

```python
import functools

import jax
import jax.numpy as jnp
import numpy as np
from jax import lax
from jax.experimental import pallas as pl
from jax.experimental.pallas import tpu as pltpu
from jax.sharding import PartitionSpec as P

MESH = pl.DeviceIdType.MESH
LAT = 512
WIDE = 576
BLK = 128
CSLOT = 256
SCALE = 192.0 ** (-0.5)
EPS = 1e-6
BIG = 1e30

ROWS = 16
NCH = BLK // ROWS
LAG = 8
SHORT = 4
EXTRA = 2
MSGS = 2 * NCH + EXTRA
SLOT = 40
PIECE = 9
SPLITS = ((0, PIECE),)
TABLE = 128


def chunk_id(block, chunk):
    half = NCH // 2
    return (chunk // half) * (4 * half) + block * half + chunk % half


def passes(rel):
    n_right, n_left = rel.count(1), rel.count(3)
    opposite = [b for b in range(4) if rel[b] == 2]
    if len(opposite) == 1:
        right = 1 if n_right <= n_left else 0
    else:
        right = 1 + (n_left == 2) - (n_right == 2)
    right = min(max(right, 0), len(opposite))
    items = [(b, j) for j in range(NCH) for b in opposite]
    if len(opposite) == 2 and right == 2:
        return items[EXTRA:], items[:EXTRA]
    if len(opposite) == 2 and right == 0:
        return items[:EXTRA], items[EXTRA:]
    return [v for v in items if v[0] in opposite[:right]], [v for v in items if v[0] in opposite[right:]]


def lane_plan(rel, side):
    near, step = (1, 1) if side == 0 else (3, -1)
    mine = passes(rel)[side]
    behind = passes([(r + step) % 4 for r in rel])[side]
    spots = {i: v + (0,) for i, v in enumerate(mine)}
    many = len(behind) > LAG
    for i, v in enumerate(behind):
        at = i + (SHORT if many else LAG)
        spots[at] = v + (2 if many else 1,)
    plain = [(b, j) for j in range(NCH) for b in range(4) if rel[b] == near and (b, j) not in behind]
    free = [m for m in range(MSGS) if m not in spots]
    spots.update({m: v + (0,) for m, v in zip(free, plain)})
    return spots


@functools.lru_cache(None)
def plan_table():
    table = np.zeros((256, TABLE), np.int32)
    for code in range(256):
        rel = [(code >> (2 * b)) & 3 for b in range(4)]
        if max(rel.count(g) for g in range(4)) > 2:
            continue
        for side in range(2):
            for m, (b, j, adds) in lane_plan(rel, side).items():
                table[code, m] |= (chunk_id(b, j) | (adds << 5)) << (7 * side)
        owned = [b for b in range(4) if rel[b] == 0]
        from_left = lane_plan([(r + 1) % 4 for r in rel], 0)
        from_right = lane_plan([(r - 1) % 4 for r in rel], 1)
        for k, b in enumerate(owned):
            for j in range(NCH):
                at_left = [m for m, v in from_left.items() if v[:2] == (b, j)][0]
                at_right = [m for m, v in from_right.items() if v[:2] == (b, j)][0]
                table[code, MSGS + k * NCH + j] = chunk_id(b, j) | (at_left << 5) | (at_right << 10)
    return table


@functools.lru_cache(None)
def turn_tables():
    lane = np.arange(128)
    inverse = 10000.0 ** (-2.0 * (lane % 32) / 64.0)
    base = (np.arange(128) * 128.0)[:, None] * inverse[None, :]
    row = np.arange(8 * NCH)
    inside = ((row // 8) * 16 + row % 8)[:, None] + np.where(lane < 64, 0, 8)[None, :]
    inside = inside * inverse[None, :]
    both = np.concatenate([np.cos(base), np.sin(base), np.cos(inside), np.sin(inside)], axis=0)
    return both.astype(np.float32)


def kernel(
    prompt, kv_down, gain, home, slot, cache, lengths, queries, news, plan, turns,
    out,
    x, w, part, send_r, send_l, recv_r, recv_l,
    gain_v, turn_v, home_s, slot_s, len_s, plan_v, row_v, plan_s,
    keys, qt, q, news_v, news_f, fresh, acc, sib, scale, metas, piece, got,
    in_sem, ss_r, ss_l, rs_r, rs_l, ss_c, rs_c, ss_a, rs_a, here,
):
    f32, bf16 = jnp.float32, jnp.bfloat16
    s = lax.axis_index("section")
    c = lax.axis_index("seq")
    core = lax.rem(c, 2)
    chip = c // 2
    y, xx, z = lax.rem(chip, 4), lax.rem(chip // 4, 4), chip // 16
    right, left = (lax.rem(s + 1, 4), c), (lax.rem(s + 3, 4), c)
    sibling = (s, chip * 2 + (1 - core))

    def at_chip(dx, dy, dz):
        to = lax.rem(z + dz, 2) * 16 + lax.rem(xx + dx, 4) * 4 + lax.rem(y + dy, 4)
        return (s, to * 2 + core)

    def tell(sem, devices):
        for device in devices:
            pl.semaphore_signal(sem, inc=1, device_id=device, device_id_type=MESH)

    x_near, y_near, z_near = [at_chip(1, 0, 0), at_chip(3, 0, 0)], [at_chip(0, 1, 0), at_chip(0, 3, 0)], [at_chip(0, 0, 1)]
    barrier = pltpu.get_barrier_semaphore()
    tell(barrier, [right, left] + x_near + y_near + z_near + [sibling])

    loads = []

    def load(src, dst):
        copy = pltpu.make_async_copy(src, dst, in_sem.at[len(loads)])
        copy.start()
        loads.append(copy)
        return copy

    first = [
        load(kv_down, w.at[pl.ds(0, WIDE)]),
        load(prompt.at[:, 0], x.at[0]),
        load(kv_down.at[pl.ds(LAT, 64)], w.at[pl.ds(WIDE, 64)]),
    ]
    small = [load(home, home_s), load(plan, plan_v)]
    second = [load(prompt.at[:, 1], x.at[1])]

    lane8 = lax.broadcasted_iota(jnp.int32, (8, 128), 1)
    lane_low = lane8 < 64

    def dot_t(a, b):
        return lax.dot_general(a, b, (((1,), (1,)), ((), ())), preferred_element_type=f32)

    def project(half):
        both = dot_t(x[half].reshape(256, x.shape[3]), w[...])
        main, turn = both[:, :LAT], both[:, LAT:]
        n = 4 * (BLK // 2) // ROWS
        main = main.reshape(n, 2, 8, LAT)
        turn = turn.reshape(n, 2, 8, 128)
        for h in range(2):
            for t in range(4):
                part[half * n : (half + 1) * n, h * 5 + t] = main[:, h, :, t * 128 : (t + 1) * 128]
        part[half * n : (half + 1) * n, 4] = jnp.where(lane_low[None], turn[:, 0], turn[:, 1])

    for copy in small:
        copy.wait()
    code = jnp.int32(0)
    for b in range(4):
        group = home_s[b] // 2
        code = code + lax.rem(group - s + 4, 4) * (4**b)
    row_v[...] = plan_v[pl.ds(code, 1)]
    row_copy = load(row_v, plan_s)

    third = [
        load(slot, slot_s),
        load(lengths, len_s),
        load(cache, keys),
        load(news, news_v),
        load(gain, gain_v),
        load(turns, turn_v),
        load(queries, qt.at[:, :, pl.ds(0, WIDE)]),
        load(queries.at[:, :, pl.ds(LAT, 64)], qt.at[:, :, pl.ds(WIDE, 64)]),
    ]
    for copy in first:
        copy.wait()
    project(0)
    row_copy.wait()
    pl.semaphore_wait(barrier, 8)
    tell(here.at[0], x_near)

    right_copies, left_copies = [], []

    def message(m):
        word = plan_s[0, m]
        for part_at, tiles in SPLITS:
            for side, (buf, got_buf, copies, ss, rs, device) in enumerate(
                (
                    (send_r, recv_r, right_copies, ss_r, rs_r, right),
                    (send_l, recv_l, left_copies, ss_l, rs_l, left),
                )
            ):
                field = word >> (7 * side)
                value = part[field & 31, pl.ds(part_at, tiles)]
                at = len(copies)
                adds = (field >> 5) & 3
                if m >= SHORT:
                    copies[m - SHORT].wait_recv()
                    value = value + jnp.where(adds == 2, got_buf[m - SHORT], 0.0)
                if m >= LAG:
                    value = value + jnp.where(adds == 1, got_buf[m - LAG], 0.0)
                buf[m, pl.ds(part_at, tiles)] = value
                copy = pltpu.make_async_remote_copy(
                    buf.at[m, pl.ds(part_at, tiles)],
                    got_buf.at[m, pl.ds(part_at, tiles)],
                    ss.at[at],
                    rs.at[at],
                    device_id=device,
                    device_id_type=MESH,
                )
                copy.start()
                copies.append(copy)

    for m in range(NCH // 2):
        message(m)
    for copy in second:
        copy.wait()
    project(1)
    for m in range(NCH // 2, LAG):
        message(m)
    pl.semaphore_wait(here.at[0], 2)
    tell(here.at[1], y_near)
    for copy in third:
        copy.wait()

    owned = jnp.int32(0)
    slot_block = [jnp.int32(0), jnp.int32(0)]
    slot_turn = [jnp.int32(0), jnp.int32(0)]
    slot_req = [jnp.int32(-1), jnp.int32(-1)]
    written = [jnp.int32(0)] * 4
    for b in range(4):
        is_mine = home_s[b] // 2 == s
        req = lax.rem(home_s[b], 2)
        target = req * 2 + slot_s[b]
        for k in range(2):
            take = is_mine & (owned == k)
            slot_req[k] = jnp.where(take, req, slot_req[k])
            slot_turn[k] = jnp.where(take, slot_s[b], slot_turn[k])
        for t in range(4):
            written[t] = jnp.where(is_mine & (target == t), 1, written[t])
        owned = owned + jnp.where(is_mine, 1, 0)

    row = lax.broadcasted_iota(jnp.int32, (256, 1), 0)
    row_req = lax.rem(row, 8) // 4
    row_new = lax.rem(row, 2)
    row_chip = row // 8

    n_keys = 2 * CSLOT + 128
    col = lax.broadcasted_iota(jnp.int32, (1, n_keys), 1)
    cblk = col // 128
    is_written = jnp.where(cblk == 0, written[0], jnp.where(cblk == 1, written[1], jnp.where(cblk == 2, written[2], written[3])))
    length = jnp.where(col < CSLOT, len_s[0], len_s[1])
    pos = c * CSLOT + lax.rem(col, CSLOT)
    col_req = jnp.where((col < 2 * CSLOT) & (pos < length) & (is_written == 0), col // CSLOT, -1)
    own_col = col - 2 * CSLOT
    own_code = jnp.where((own_col >= 0) & (own_col < 4), own_col, -9)

    def order_queries(half):
        i = lax.broadcasted_iota(jnp.int32, (256, 1), 0)
        head = (i // 8) * 4 + half * 2 + lax.rem(i // 2, 2)
        pick = lax.broadcasted_iota(jnp.int32, (256, 128), 1)
        rows = jnp.zeros((256, 640), f32)
        for r in range(2):
            for n in range(2):
                wanted = jnp.where((lax.rem(i // 4, 2) == r) & (lax.rem(i, 2) == n), head, -1)
                rows = rows + dot_t(jnp.where(pick == wanted, 1.0, 0.0).astype(bf16), qt[r, n])
        q[half] = rows.astype(bf16)

    def old_part(half):
        rows = q[half, :, :WIDE]
        scores = jnp.concatenate(
            [
                jnp.dot(rows, keys[0], preferred_element_type=f32),
                jnp.dot(rows, keys[1], preferred_element_type=f32),
                dot_t(rows, news_f[...].astype(bf16)),
            ],
            axis=1,
        )
        scores = scores * SCALE
        here = jnp.where((half == core) & (row_chip == chip), 1, 0)
        mask = (col_req == row_req) | (
            (own_code // 2 == row_req) & (lax.rem(own_code, 2) <= row_new) & (own_code >= 0) & (here == 1)
        )
        top = jnp.max(jnp.where(mask, scores, -BIG), axis=1, keepdims=True)
        weight = jnp.where(mask, jnp.exp(scores - top), 0.0).astype(bf16)
        total = jnp.sum(weight.astype(f32), axis=1, keepdims=True)
        acc[half, :, :LAT] = (
            dot_t(weight[:, :CSLOT], keys[0, :LAT])
            + dot_t(weight[:, CSLOT : 2 * CSLOT], keys[1, :LAT])
            + jnp.dot(weight[:, 2 * CSLOT :], news_f[:, :LAT].astype(bf16), preferred_element_type=f32)
        )
        lanes = lax.broadcasted_iota(jnp.int32, (256, 128), 1)
        acc[half, :, LAT:] = jnp.where(lanes < 64, total, top)

    news_f[...] = jnp.zeros_like(news_f)
    for r in range(2):
        news_f[2 * r : 2 * r + 2] = news_v[r].astype(f32)
    message(LAG)
    order_queries(1 - core)
    message(LAG + 1)
    order_queries(core)
    message(LAG + 2)
    old_part(1 - core)
    pl.semaphore_wait(here.at[1], 2)
    tell(here.at[2], y_near)
    message(LAG + 3)
    old_part(core)
    for m in range(LAG + 4, LAG + 6):
        message(m)
    pl.semaphore_wait(here.at[2], 2)
    tell(here.at[3], z_near)
    for m in range(LAG + 6, MSGS):
        message(m)
    pl.semaphore_wait(here.at[3], 1)
    for at in range(MSGS - SHORT, MSGS):
        right_copies[at].wait_recv()
        left_copies[at].wait_recv()

    sign = jnp.where(lax.rem(lane8, 64) < 32, -1.0, 1.0)
    near_half = lax.rem(lane8, 64) < 32
    gain_row = gain_v[...]
    for k in range(2):
        turn_at = c * 2 + slot_turn[k]
        cos_b = turn_v[pl.ds(turn_at, 1)]
        sin_b = turn_v[pl.ds(turn_at + 128, 1)]
        for j in range(NCH):
            word = plan_s[0, MSGS + k * NCH + j]
            value = part[word & 31] + recv_r[(word >> 5) & 31] + recv_l[(word >> 10) & 31]
            for h in range(2):
                pieces = [value[h * 5 + t] for t in range(4)]
                square = pieces[0] * pieces[0]
                for t in range(1, 4):
                    square = square + pieces[t] * pieces[t]
                factor = lax.rsqrt(jnp.sum(square, axis=1, keepdims=True) * (1.0 / LAT) + EPS)
                pieces = [p * factor * gain_row[:, t * 128 : (t + 1) * 128] for t, p in enumerate(pieces)]
                if h == 0:
                    upper = pieces
            cos_i = turn_v[256 + j * 8 : 256 + (j + 1) * 8]
            sin_i = turn_v[320 + j * 8 : 320 + (j + 1) * 8]
            cosine = cos_b * cos_i - sin_b * sin_i
            sine = (sin_b * cos_i + cos_b * sin_i) * sign
            rotary = value[4]
            swapped = jnp.where(near_half, pltpu.roll(rotary, 96, 1), pltpu.roll(rotary, 32, 1))
            turned = rotary * cosine + swapped * sine
            at = k * BLK + j * ROWS
            for t in range(4):
                fresh[at : at + ROWS, t * 128 : (t + 1) * 128] = jnp.concatenate([upper[t], pieces[t]], axis=0).astype(bf16)
            fresh[at : at + ROWS, LAT:] = jnp.concatenate(
                [jnp.where(lane_low, turned, 0.0), jnp.where(lane_low, 0.0, turned)], axis=0
            ).astype(bf16)

    fcol = lax.broadcasted_iota(jnp.int32, (1, 2 * BLK), 1)
    fresh_req = jnp.where(fcol < BLK, slot_req[0], slot_req[1])

    low = lax.broadcasted_iota(jnp.int32, (128, 128), 1) < 64

    def rows_of(plane):
        return pl.ds(pl.multiple_of(plane * 128, 128), 128)

    def new_part(half, plane):
        rows = rows_of(plane)
        scores = dot_t(q[half, rows], fresh[...]) * SCALE
        mask = fresh_req == row_req[:128]
        old_total = acc[half, rows, LAT : LAT + 1]
        old_top = acc[half, rows, LAT + 64 : LAT + 65]
        top = jnp.maximum(jnp.max(jnp.where(mask, scores, -BIG), axis=1, keepdims=True), old_top)
        weight = jnp.where(mask, jnp.exp(scores - top), 0.0).astype(bf16)
        shrink = jnp.exp(old_top - top)
        total = jnp.sum(weight.astype(f32), axis=1, keepdims=True) + old_total * shrink
        acc[half, rows, :LAT] = acc[half, rows, :LAT] * shrink + jnp.dot(
            weight, fresh[:, :LAT], preferred_element_type=f32
        )
        acc[half, rows, LAT:] = jnp.where(low, total, top)

    planes = (1 - z, z)
    swaps = []
    for k, plane in enumerate(planes):
        new_part(1 - core, plane)
        swap = pltpu.make_async_remote_copy(
            acc.at[1 - core, rows_of(plane)], sib.at[rows_of(plane)], ss_c.at[k], rs_c.at[k],
            device_id=sibling, device_id_type=MESH,
        )
        swap.start()
        swaps.append(swap)
    for plane in planes:
        new_part(core, plane)

    lanes = lax.broadcasted_iota(jnp.int32, (128, 128), 1)
    spot = lax.rem(lax.broadcasted_iota(jnp.int32, (128, 128), 0), 8)

    def merge_scales(plane):
        rows = rows_of(plane)
        meta_a, meta_b = acc[core, rows, LAT:], sib[rows, LAT:]
        total_a, total_b = meta_a[:, :1], meta_b[:, :1]
        top_a, top_b = meta_a[:, 64:65], meta_b[:, 64:65]
        top = jnp.maximum(top_a, top_b)
        fa, fb = jnp.exp(top_a - top), jnp.exp(top_b - top)
        scale[0, rows] = jnp.broadcast_to(fa, (128, 128))
        scale[1, rows] = jnp.broadcast_to(fb, (128, 128))
        meta = jnp.where(lanes == spot, total_a * fa + total_b * fb, jnp.where(lanes == spot + 8, top, 0.0))
        metas[pl.ds(pl.multiple_of(plane * 16, 16), 16)] = jnp.sum(meta.reshape(16, 8, 128), axis=1)

    def hops(i):
        dx, dy = (i // 4) % 4, i % 4
        return i // 16 + min(dx, 4 - dx) + min(dy, 4 - dy)

    order = sorted(range(16, 32), key=hops, reverse=True) + sorted(range(16), key=hops, reverse=True)
    for at, i in enumerate(order):
        if at % 16 == 0:
            swaps[at // 16].wait_recv()
            merge_scales(planes[at // 16])
        _, to = at_chip((i // 4) % 4, i % 4, i // 16)
        to = to // 2
        rows = pl.ds(pl.multiple_of(to * 8, 8), 8)
        store = piece if i else got
        fa, fb = scale[0, rows], scale[1, rows]
        for t in range(4):
            cols = slice(t * 128, (t + 1) * 128)
            store[i * SLOT + t * 8 : i * SLOT + (t + 1) * 8] = acc[core, rows, cols] * fa + sib[rows, cols] * fb
        store[i * SLOT + 32 : i * SLOT + 33] = metas[pl.ds(to, 1)]
        if i:
            pltpu.make_async_remote_copy(
                piece.at[pl.ds(i * SLOT, 33)], got.at[pl.ds(i * SLOT, 33)], ss_a, rs_a,
                device_id=(s, to * 2 + core), device_id_type=MESH,
            ).start()

    for swap in swaps:
        swap.wait_send()
    for copy in right_copies + left_copies:
        copy.wait_send()
    every = pltpu.make_async_remote_copy(
        piece.at[pl.ds(0, 31 * 33)], got.at[pl.ds(0, 31 * 33)], ss_a, rs_a, device_id=sibling, device_id_type=MESH
    )
    every.wait_recv()
    every.wait_send()

    meta = got[pl.ds(32, 32, stride=SLOT)]
    share = pltpu.roll(jnp.exp(meta - jnp.max(meta, axis=0, keepdims=True)), 120, 1)
    diagonal = lane8 == lax.broadcasted_iota(jnp.int32, (8, 128), 0)

    def column(line):
        return jnp.sum(jnp.where(diagonal, line, 0.0), axis=1, keepdims=True)

    total = column(jnp.sum(meta * share, axis=0, keepdims=True))
    number = [jnp.zeros((8, 128), f32)] * 4
    for i in range(32):
        factor = column(share[i : i + 1])
        number = [v + got[i * SLOT + t * 8 : i * SLOT + (t + 1) * 8] * factor for t, v in enumerate(number)]
    inverse = 1.0 / total
    out[...] = jnp.concatenate([v * inverse for v in number], axis=1).astype(bf16)


def body(prompt, kv_down, latent_gain, block_home, block_slot, latent_cache, cache_lengths, queries, new_rows):
    f32, bf16 = jnp.float32, jnp.bfloat16
    any_space = pl.BlockSpec(memory_space=pl.ANY)
    n_loads = 15
    dma = pltpu.SemaphoreType.DMA
    msg = (PIECE, 8, 128)
    out = pl.pallas_call(
        kernel,
        out_shape=jax.ShapeDtypeStruct((8, LAT), bf16),
        in_specs=[any_space] * 11,
        out_specs=pl.BlockSpec(memory_space=pltpu.VMEM),
        scratch_shapes=[
            pltpu.VMEM((2, 4, BLK // 2, prompt.shape[1]), bf16),
            pltpu.VMEM((640, kv_down.shape[0]), bf16),
            pltpu.VMEM((4 * NCH,) + msg, f32),
            pltpu.VMEM((MSGS,) + msg, f32),
            pltpu.VMEM((MSGS,) + msg, f32),
            pltpu.VMEM((MSGS,) + msg, f32),
            pltpu.VMEM((MSGS,) + msg, f32),
            pltpu.VMEM((1, LAT), f32),
            pltpu.VMEM((384, 128), f32),
            pltpu.SMEM((4,), jnp.int32),
            pltpu.SMEM((4,), jnp.int32),
            pltpu.SMEM((2,), jnp.int32),
            pltpu.VMEM((256, TABLE), jnp.int32),
            pltpu.VMEM((1, TABLE), jnp.int32),
            pltpu.SMEM((1, TABLE), jnp.int32),
            pltpu.VMEM((2, WIDE, CSLOT), bf16),
            pltpu.VMEM((2, 2, 640, 128), bf16),
            pltpu.VMEM((2, 256, 640), bf16),
            pltpu.VMEM((2, 2, WIDE), bf16),
            pltpu.VMEM((128, WIDE), f32),
            pltpu.VMEM((2 * BLK, 640), bf16),
            pltpu.VMEM((2, 256, 640), f32),
            pltpu.VMEM((256, 640), f32),
            pltpu.VMEM((2, 256, 128), f32),
            pltpu.VMEM((32, 128), f32),
            pltpu.VMEM((32 * SLOT, 128), f32),
            pltpu.VMEM((32 * SLOT, 128), f32),
            dma((n_loads,)),
            dma((MSGS * len(SPLITS),)),
            dma((MSGS * len(SPLITS),)),
            dma((MSGS * len(SPLITS),)),
            dma((MSGS * len(SPLITS),)),
            dma((2,)),
            dma((2,)),
            dma,
            dma,
            pltpu.SemaphoreType.REGULAR((4,)),
        ],
        compiler_params=pltpu.CompilerParams(
            collective_id=0, has_side_effects=True, vmem_limit_bytes=62 * 1024 * 1024
        ),
        name="mla_decode",
    )(
        prompt.reshape(4, 2, BLK // 2, prompt.shape[1]), kv_down.T, latent_gain.reshape(1, LAT), block_home, block_slot, latent_cache.transpose(0, 2, 1),
        cache_lengths, queries.transpose(0, 2, 3, 1), new_rows,
        jnp.asarray(plan_table()), jnp.asarray(turn_tables()),
    )
    return out.reshape(2, 2, 2, LAT)


def solution(mesh):
    placed = (
        P("seq", "section"),
        P("section", None),
        P(),
        P("seq"),
        P("seq"),
        P("section", "seq", None),
        P("section"),
        P("section", None, None, None),
        P("section", None, None),
    )
    return jax.shard_map(body, mesh=mesh, in_specs=placed, out_specs=P("section", "seq", None, None), check_vma=False)
```
